32 devices in a mesh: dp: 4 (over z), expert: 8 (over y, x, core).
Axes of the slice: x: 2, y: 2, z: 4, core: 2. Of those that a mesh axis runs over, the one named last changes fastest.
Arguments:
- tokens: bfloat16 [128, 197, 768], P(('dp', 'expert')), may hold values from -6 to 6
- routes: int32 [128, 197, 2], P(('dp', 'expert')), may hold values from 0 to 7, all different within a row; in each aligned block of 788 rows (0 to 787, 788 to 1575, ..., all dimensions but the last counted through in order) at most 248 rows name the same one
- gain_one: bfloat16 [768], P(('dp', 'expert')), may hold values from 0.5 to 1.5
- shift_one: bfloat16 [768], P(('dp', 'expert')), may hold values from -1.796875 to 1.796875
- w_query: bfloat16 [768, 768], P(('dp', 'expert')), may hold values from -0.21875 to 0.21875
- b_query: bfloat16 [768], P(('dp', 'expert')), may hold values from -1.796875 to 1.796875
- w_key: bfloat16 [768, 768], P(('dp', 'expert')), may hold values from -0.21875 to 0.21875
- w_value: bfloat16 [768, 768], P(('dp', 'expert')), may hold values from -0.21875 to 0.21875
- b_value: bfloat16 [768], P(('dp', 'expert')), may hold values from -1.796875 to 1.796875
- w_out: bfloat16 [768, 768], P(('dp', 'expert')), may hold values from -1.75 to 1.75
- b_out: bfloat16 [768], P(('dp', 'expert')), may hold values from -1.796875 to 1.796875
- gain_two: bfloat16 [768], P(('dp', 'expert')), may hold values from 0.5 to 1.5
- shift_two: bfloat16 [768], P(('dp', 'expert')), may hold values from -1.796875 to 1.796875
- w_router: bfloat16 [768, 8], P(('dp', 'expert')), may hold values from -0.15625 to 0.15625
- w_up: bfloat16 [8, 768, 3072], P('expert'), may hold values from -0.21875 to 0.21875
- b_up: bfloat16 [8, 3072], P('expert'), may hold values from -0.59765625 to 0.59765625
- w_down: bfloat16 [8, 3072, 768], P('expert'), may hold values from -2.390625 to 2.390625
- b_down: bfloat16 [8, 768], P('expert'), may hold values from -9 to 9
- cotangent: bfloat16 [128, 197, 768], P(('dp', 'expert')), may hold values from -6 to 6
Outputs:
- mixed: bfloat16 [128, 197, 768], P(('dp', 'expert'))
- grad_tokens: float32 [128, 197, 768], P(('dp', 'expert'))
- grad_gain_one: float32 [768], P(('dp', 'expert'))
- grad_shift_one: float32 [768], P(('dp', 'expert'))
- grad_w_query: float32 [768, 768], P(('dp', 'expert'))
- grad_b_query: float32 [768], P(('dp', 'expert'))
- grad_w_key: float32 [768, 768], P(('dp', 'expert'))
- grad_w_value: float32 [768, 768], P(('dp', 'expert'))
- grad_b_value: float32 [768], P(('dp', 'expert'))
- grad_w_out: float32 [768, 768], P(('dp', 'expert'))
- grad_b_out: float32 [768], P(('dp', 'expert'))
- grad_gain_two: float32 [768], P(('dp', 'expert'))
- grad_shift_two: float32 [768], P(('dp', 'expert'))
- grad_w_router: float32 [768, 8], P(('dp', 'expert'))
- grad_w_up: float32 [8, 768, 3072], P('expert', 'dp')
- grad_b_up: float32 [8, 3072], P('expert', 'dp')
- grad_w_down: float32 [8, 3072, 768], P('expert', 'dp')
- grad_b_down: float32 [8, 768], P('expert', 'dp')
The draws below stay inside these ranges and needn't reach their ends.
Inputs may be any that keep to these rules, and one draw needn't show every extreme that they name: `routes`: the two experts of a token differ. Among the rows of one device no expert is named more than 248 times, and in every draw some expert is named exactly 248 times by the rows of some device.
All inputs are finite; a program needn't handle non-finite values.
Results may differ from the reference program's by a relative error of at most 0.015.
Values may be sent and summed in bfloat16 or wider, within the bound.
No kernel may reach another device: no remote copies, remote signals or barrier semaphores. Data moves between devices by JAX's collectives and lax.ppermute only.
A program may use at most 256 MiB of HBM per device.

```python
import math
import jax
import jax.numpy as jnp
import numpy as np
from jax import lax

D = 768
HEADS = 12
HEAD_DIM = 64
FF = 3072
SEQ = 197
IMG_DEV = 4
TOK_DEV = 788
IMAGES = 128
EXPERTS = 8
CAP = 248
DEVICES = 32


def block_scale(own_key, extent, pieces, smallest, largest):
    def one(dim, shards_of):
        steps = jax.random.uniform(jax.random.fold_in(jax.random.fold_in(own_key, 6), dim), (shards_of,), jnp.float32, smallest / len(pieces), largest / len(pieces))
        return jnp.repeat(jnp.exp(steps), extent[dim] // shards_of).reshape((-1,) + (1,) * (len(extent) - dim - 1))

    level = one(*pieces[0])
    for cut in pieces[1:]:
        level = level * one(*cut)
    return level


def routed_block(stream_key, own, number, rows, count, top, reach, slope):
    ranking = jax.random.permutation(stream_key, count)
    heavy_load, usual = portions_of(count, rows * top, reach, slope, True), portions_of(count, rows * top, reach, slope, False)
    places = jnp.arange(count)

    def named(lengths, turn):
        used = int((lengths > 0).sum())
        fixed = max(1, used // 4)
        moved = fixed + (places - fixed + turn * (used - fixed)) % max(1, count - fixed)
        return jnp.zeros((count,), jnp.int32).at[ranking[jnp.where(places < fixed, places, moved)]].set(jnp.asarray(lengths, jnp.int32))

    lengths = jnp.where(number % 4 == 0, named(heavy_load, number // 4), named(usual, number - number // 4 - 1))
    mixed = jax.random.permutation(jax.random.fold_in(own, 3), count)
    donor, taker = mixed[0:count // 2 * 2:2], mixed[1:count // 2 * 2:2]
    slack = jnp.minimum(lengths[donor] - 1, reach - lengths[taker]) // 2
    slack = jnp.where((donor == ranking[0]) | (taker == ranking[0]) | (lengths[taker] == 0), 0, jnp.maximum(slack, 0))
    moved = jax.random.randint(jax.random.fold_in(own, 4), (count // 2,), 0, 1 << 20) % (slack + 1)
    lengths = lengths.at[donor].add(-moved).at[taker].add(moved)
    labels = jnp.searchsorted(jnp.cumsum(lengths), jnp.arange(rows * top), side="right").astype(jnp.int32)
    listing = labels.reshape(top, rows).T
    listing = listing[jax.random.permutation(jax.random.fold_in(own, 1), rows)]
    turn = jax.random.randint(jax.random.fold_in(own, 2), (rows, 1), 0, top)
    return jnp.take_along_axis(listing, (jnp.arange(top)[None, :] + turn) % top, axis=1)


def portions_of(amount, total, bound, slope, full):
    weights = [(1 << 20) // math.isqrt(rank ** slope) + 1 for rank in range(1, amount + 1)]
    largest = bound if full else min(bound, max(-(-total // amount), total * weights[0] // sum(weights)))
    least = 1 if total - largest >= amount - 1 else 0
    holding, rest = [largest] + [least] * (amount - 1), total - largest - least * (amount - 1)
    while rest > 0:
        candidates = [i for i in range(1, amount) if holding[i] < largest] or [i for i in range(1, amount) if holding[i] < bound]
        whole, budget = sum([weights[i] for i in candidates]), rest
        for i in candidates:
            addition = min(bound - holding[i], max(1, budget * weights[i] // whole), rest)
            holding[i] = holding[i] + addition
            rest = rest - addition
    return np.array(holding)


def gaussian(own_key, extent, scale, most, shards=(), kind=jnp.bfloat16):
    level = block_scale(own_key, extent, shards, -0.22, 0.18) if shards else 1.0
    array = jax.random.normal(own_key, extent, jnp.float32) * scale * level
    return jnp.minimum(jnp.maximum(array, -most), most).astype(kind)


def setup_inputs(seed: int = 0) -> dict:
    splits = jax.random.split(jax.random.key(seed), 20)
    tokens = gaussian(splits[0], (IMAGES, SEQ, D), 1.0, 6.0, ((0, 32),))
    routes_keys = jax.random.split(jax.random.fold_in(splits[1], 1), IMAGES * SEQ // TOK_DEV)
    routes_turns = jax.random.permutation(jax.random.fold_in(splits[1], 3), IMAGES * SEQ // TOK_DEV)
    routes = jax.vmap(lambda own, number: routed_block(jax.random.fold_in(splits[1], 2), own, number, TOK_DEV, EXPERTS, 2, CAP, 1))(routes_keys, routes_turns).reshape((IMAGES, SEQ, 2))
    gain_one = jnp.clip(1.0 + 0.1 * jax.random.normal(splits[2], (D,), jnp.float32), 0.5, 1.5).astype(jnp.bfloat16)
    shift_one = gaussian(splits[3], (D,), 0.3, 1.796875, ((0, 32),))
    w_query = gaussian(splits[4], (D, D), D ** -0.5, 0.21875, ((0, 32),))
    b_query = gaussian(splits[5], (D,), 0.3, 1.796875, ((0, 32),))
    w_key = gaussian(splits[6], (D, D), D ** -0.5, 0.21875, ((0, 32),))
    w_value = gaussian(splits[7], (D, D), D ** -0.5, 0.21875, ((0, 32),))
    b_value = gaussian(splits[8], (D,), 0.3, 1.796875, ((0, 32),))
    w_out = gaussian(splits[9], (D, D), (D // 64) ** -0.5, 1.75, ((0, 32),))
    b_out = gaussian(splits[10], (D,), 0.3, 1.796875, ((0, 32),))
    gain_two = jnp.clip(1.0 + 0.1 * jax.random.normal(splits[11], (D,), jnp.float32), 0.5, 1.5).astype(jnp.bfloat16)
    shift_two = gaussian(splits[12], (D,), 0.3, 1.796875, ((0, 32),))
    w_router = gaussian(splits[13], (D, EXPERTS), (2 * D) ** -0.5, 0.15625, ((0, 32),))
    w_up = gaussian(splits[14], (EXPERTS, D, FF), D ** -0.5, 0.21875, ((0, 8),))
    b_up = gaussian(splits[15], (EXPERTS, FF), 0.1, 0.59765625, ((0, 8),))
    w_down = gaussian(splits[16], (EXPERTS, FF, D), 0.4, 2.390625, ((0, 8),))
    b_down = gaussian(splits[17], (EXPERTS, D), 1.5, 9.0, ((0, 8),))
    cotangent = gaussian(splits[18], (IMAGES, SEQ, D), 1.0, 6.0, ((0, 32),))
    return dict(tokens=tokens, routes=routes, gain_one=gain_one, shift_one=shift_one, w_query=w_query, b_query=b_query, w_key=w_key, w_value=w_value, b_value=b_value, w_out=w_out, b_out=b_out, gain_two=gain_two, shift_two=shift_two, w_router=w_router, w_up=w_up, b_up=b_up, w_down=w_down, b_down=b_down, cotangent=cotangent)


@jax.custom_vjp
def low(v):
    return lax.optimization_barrier(v.astype(jnp.bfloat16)).astype(jnp.float32)

@jax.custom_vjp
def low_back(v):
    return v

def low_keep(v):
    return (low(v), None)

def low_pass(kept, grad):
    return (grad,)

def back_keep(v):
    return (v, None)

def back_low(kept, grad):
    return (low(grad),)
low.defvjp(low_keep, low_pass)
low_back.defvjp(back_keep, back_low)
highest = lax.Precision.HIGHEST
epsilon = 1e-06

def layer_norm(values, gain, shift):
    center = values - lax.optimization_barrier(jnp.mean(values, axis=-1, keepdims=True))
    spread = lax.optimization_barrier(jnp.mean(center * center, axis=-1, keepdims=True))
    return center * lax.rsqrt(spread + epsilon) * gain + shift

def block_forward(params, inputs, routes_block):
    gain_one, shift_one, w_query, b_query, w_key, w_value, b_value, w_out, b_out, gain_two, shift_two, w_router, w_up, b_up, w_down, b_down = params
    images = inputs.shape[0]
    rows = images * SEQ
    heads_shape = (images, SEQ, HEADS, HEAD_DIM)
    scale = HEAD_DIM ** (-0.5)
    flat = inputs.reshape(rows, D)
    normed = low(layer_norm(flat, gain_one, shift_one))
    query = low(low_back(jnp.dot(normed, w_query, precision=highest) + b_query))
    key = low(low_back(jnp.dot(normed, w_key, precision=highest)))
    value = low(low_back(jnp.dot(normed, w_value, precision=highest) + b_value))
    scores = low_back(jnp.einsum('bqhd,bkhd->bhqk', query.reshape(heads_shape), key.reshape(heads_shape), precision=highest) * scale)
    probs = low(jax.nn.softmax(scores, axis=-1))
    attended = jnp.einsum('bhqk,bkhd->bqhd', probs, value.reshape(heads_shape), precision=highest).reshape(rows, D)
    attended = low(low_back(attended))
    branch = low_back(jnp.dot(attended, w_out, precision=highest) + b_out)
    resid = flat + branch
    normed_two = low(layer_norm(resid, gain_two, shift_two))
    logits = jnp.dot(normed_two, w_router, precision=highest)
    gates = jax.nn.softmax(logits, axis=-1)
    flat_routes = routes_block.reshape(-1).astype(jnp.int32)
    table = (flat_routes[:, None] == jnp.arange(EXPERTS, dtype=jnp.int32)[None, :]).astype(jnp.int32)
    before = (jnp.cumsum(table, axis=0) - table).astype(jnp.int32)
    slot = lax.optimization_barrier(jnp.sum(before * table, axis=1)).astype(jnp.int32)
    position = (flat_routes * CAP + slot).astype(jnp.int32)
    picks = lax.optimization_barrier(jnp.sum(jnp.repeat(gates, 2, axis=0) * table.astype(jnp.float32), axis=1))
    entering = low_back(jnp.repeat(normed_two, 2, axis=0))
    buffer = jnp.zeros((EXPERTS * CAP, D), jnp.float32).at[position].set(entering).reshape(EXPERTS, CAP, D)
    hidden = low_back(jnp.einsum('ecd,edf->ecf', buffer, w_up, precision=highest) + b_up[:, None, :])
    active = low(jax.nn.gelu(hidden, approximate=False))
    result = jnp.einsum('ecf,efd->ecd', active, w_down, precision=highest) + b_down[:, None, :]
    result = low(low_back(result)).reshape(EXPERTS * CAP, D)
    picked = result[position] * picks[:, None]
    mixed = resid + lax.optimization_barrier(jnp.sum(picked.reshape(rows, 2, D), axis=1))
    return mixed.reshape(images, SEQ, D)

def forward(params, inputs, routes):
    blocks_in = inputs.reshape(DEVICES, IMG_DEV, SEQ, D)
    blocks_routes = routes.reshape(DEVICES, TOK_DEV, 2)
    stepper = jax.checkpoint(block_forward)

    def scan_body(carry, pair):
        return (carry, stepper(params, pair[0], pair[1]))
    unused, outputs = lax.scan(scan_body, jnp.zeros((), jnp.float32), (blocks_in, blocks_routes))
    return outputs.reshape(IMAGES, SEQ, D)

def reference(tokens, routes, gain_one, shift_one, w_query, b_query, w_key, w_value, b_value, w_out, b_out, gain_two, shift_two, w_router, w_up, b_up, w_down, b_down, cotangent):
    weights = tuple((weight_array.astype(jnp.float32) for weight_array in (gain_one, shift_one, w_query, b_query, w_key, w_value, b_value, w_out, b_out, gain_two, shift_two, w_router, w_up, b_up, w_down, b_down)))
    output, pullback = jax.vjp(lambda params, inputs: forward(params, inputs, routes), weights, tokens.astype(jnp.float32))
    grads, grad_tokens = pullback(cotangent.astype(jnp.float32))
    return (output.astype(jnp.bfloat16), grad_tokens, grads[0], grads[1], grads[2], grads[3], grads[4], grads[5], grads[6], grads[7], grads[8], grads[9], grads[10], grads[11], grads[12], grads[13], grads[14], grads[15])
```

```python
import functools

import jax
import jax.numpy as jnp
from jax import lax
from jax.experimental import pallas as pl
from jax.experimental.pallas import tpu as pltpu
from jax.sharding import PartitionSpec as P

HEADS = 12
HEAD_DIM = 64
PAIR = 2 * HEAD_DIM
EPSILON = 1e-06
SCALE = HEAD_DIM**-0.5
HIGHEST = lax.Precision.HIGHEST
VMEM_LIMIT = 60 * 1024 * 1024
BF16 = jnp.bfloat16
F32 = jnp.float32


def round_up(value, unit):
    return -(-value // unit) * unit


def dot(left, right):
    return jnp.dot(left, right, preferred_element_type=F32)


def dot_nt(left, right):
    return lax.dot_general(left, right, (((1,), (1,)), ((), ())), preferred_element_type=F32)


def dot_tn(left, right):
    return lax.dot_general(left, right, (((0,), (0,)), ((), ())), preferred_element_type=F32)


def params(grid_dims=1):
    return pltpu.CompilerParams(
        vmem_limit_bytes=VMEM_LIMIT, dimension_semantics=("arbitrary",) * grid_dims
    )


def whole(shape):
    zeros = (0,) * len(shape)
    return pl.BlockSpec(shape, lambda *_: zeros, pipeline_mode=pl.Buffered(1))


def per_image(*shape):
    zeros = (0,) * len(shape)
    return pl.BlockSpec((1,) + shape, lambda i: (i,) + zeros)


def norm_parts(values):
    center = values - jnp.mean(values, axis=-1, keepdims=True)
    inverse = lax.rsqrt(jnp.mean(center * center, axis=-1, keepdims=True) + EPSILON)
    return center * inverse, inverse


def norm_pull(unit, inverse, gain, grad):
    scaled = grad * gain
    return (
        scaled
        - jnp.mean(scaled, axis=-1, keepdims=True)
        - unit * jnp.mean(scaled * unit, axis=-1, keepdims=True)
    ) * inverse


def stack_heads(pair):
    low_half = lax.broadcasted_iota(jnp.int32, pair.shape, 1) < HEAD_DIM
    zero = jnp.zeros_like(pair)
    return jnp.concatenate(
        [jnp.where(low_half, pair, zero), jnp.where(low_half, zero, pair)], axis=0
    )


def merge_heads(stacked):
    rows = stacked.shape[0] // 2
    low_half = lax.broadcasted_iota(jnp.int32, (rows, PAIR), 1) < HEAD_DIM
    return jnp.where(low_half, stacked[:rows], stacked[rows:])


def pair_probs(query_stack, key_pair, seq_len):
    scores = dot_nt(query_stack, key_pair) * SCALE
    column = lax.broadcasted_iota(jnp.int32, scores.shape, 1)
    scores = jnp.where(column < seq_len, scores, -1e30)
    powers = jnp.exp(scores - jnp.max(scores, axis=1, keepdims=True))
    return powers * (1.0 / jnp.sum(powers, axis=1, keepdims=True))


def forward_kernel(
    seq_len,
    x_ref,
    wq_ref,
    wk_ref,
    wv_ref,
    wo_ref,
    vec_ref,
    router_ref,
    q_ref,
    k_ref,
    v_ref,
    att_ref,
    resid_ref,
    low_ref,
    gates_ref,
    gates_t_ref,
):
    x = x_ref[0].astype(F32)
    unit, _ = norm_parts(x)
    normed = (unit * vec_ref[0:1] + vec_ref[1:2]).astype(BF16)
    q_ref[0] = (dot(normed, wq_ref[...]) + vec_ref[2:3]).astype(BF16)
    k_ref[0] = dot(normed, wk_ref[...]).astype(BF16)
    v_ref[0] = (dot(normed, wv_ref[...]) + vec_ref[3:4]).astype(BF16)
    for j in range(HEADS // 2):
        cols = slice(j * PAIR, (j + 1) * PAIR)
        probs = pair_probs(stack_heads(q_ref[0, :, cols]), k_ref[0, :, cols], seq_len)
        mixed = merge_heads(dot(probs.astype(BF16), v_ref[0, :, cols]))
        att_ref[0, :, cols] = mixed.astype(BF16)
    resid = x + dot(att_ref[0], wo_ref[...]) + vec_ref[4:5]
    resid_ref[0] = resid
    unit_two, _ = norm_parts(resid)
    low = (unit_two * vec_ref[5:6] + vec_ref[6:7]).astype(BF16)
    low_ref[0] = low
    logits = dot(low, router_ref[...])
    powers = jnp.exp(logits - jnp.max(logits, axis=1, keepdims=True))
    gates = powers * (1.0 / jnp.sum(powers, axis=1, keepdims=True))
    gates_ref[0] = gates
    gates_t_ref[0] = gates.T


def run_forward(tokens, first, second, vectors, router, seq_len):
    images, rows, width = tokens.shape
    experts = router.shape[1]

    def column(j):
        return pl.BlockSpec((width, width), lambda i: (0, j), pipeline_mode=pl.Buffered(1))

    big = jax.ShapeDtypeStruct((images, rows, width), BF16)
    return pl.pallas_call(
        functools.partial(forward_kernel, seq_len),
        grid=(images,),
        in_specs=[
            per_image(rows, width),
            column(0),
            column(1),
            column(0),
            column(1),
            whole(vectors.shape),
            whole(router.shape),
        ],
        out_specs=[per_image(rows, width)] * 6
        + [per_image(rows, experts), per_image(experts, rows)],
        out_shape=[big, big, big, big, jax.ShapeDtypeStruct(big.shape, F32), big]
        + [
            jax.ShapeDtypeStruct((images, rows, experts), F32),
            jax.ShapeDtypeStruct((images, experts, rows), F32),
        ],
        compiler_params=params(),
        cost_estimate=pl.CostEstimate(
            flops=10 * images * rows * width * width, bytes_accessed=20_000_000, transcendentals=0
        ),
    )(tokens, first, first, second, second, vectors, router)


def dispatch_kernel(capacity, pos_ref, values_ref, *rest):
    gates_t_ref = rest[0] if len(rest) == 2 else None
    out_ref = rest[-1]
    expert = pl.program_id(0)
    images, rows, width = values_ref.shape
    slots = out_ref.shape[1]
    lanes = round_up(slots, 128)
    total = jnp.zeros((slots, width), F32)
    parts = jnp.zeros((8, lanes), F32)
    index = lax.broadcasted_iota(jnp.int32, (lanes, rows), 0)
    slot = jnp.where(index < slots, index + expert * slots, -2)
    for b in range(images):
        hit = (pos_ref[b, 0:1] == slot) | (pos_ref[b, 1:2] == slot)
        hit = jnp.where(hit, 1.0, 0.0).astype(BF16)
        total = total + dot(hit[:slots], values_ref[b])
        if gates_t_ref is not None:
            gate = jnp.broadcast_to(gates_t_ref[b, pl.ds(expert, 1)], (8, rows))
            high = gate.astype(BF16).astype(F32)
            middle = (gate - high).astype(BF16).astype(F32)
            part = lax.broadcasted_iota(jnp.int32, gate.shape, 0)
            split = jnp.where(
                part == 0,
                high,
                jnp.where(part == 1, middle, jnp.where(part == 2, gate - high - middle, 0.0)),
            )
            parts = parts + dot_nt(split.astype(BF16), hit)
    if gates_t_ref is not None:
        tail = jnp.concatenate([parts, jnp.zeros((8, width - lanes), F32)], axis=1)
        pieces = [total[:capacity], tail]
        if slots > capacity + 8:
            pieces.append(total[capacity + 8 :])
        total = jnp.concatenate(pieces, axis=0)
    out_ref[0] = total.astype(BF16)


def run_dispatch(pos_rows, values, capacity, slots, experts, gates_t=None):
    width = values.shape[2]
    operands = (pos_rows, values) + (() if gates_t is None else (gates_t,))
    return pl.pallas_call(
        functools.partial(dispatch_kernel, capacity),
        grid=(experts,),
        in_specs=[whole(o.shape) for o in operands],
        out_specs=pl.BlockSpec((1, slots, width), lambda i: (i, 0, 0)),
        out_shape=jax.ShapeDtypeStruct((experts, slots, width), BF16),
        compiler_params=params(),
        cost_estimate=pl.CostEstimate(
            flops=2 * experts * slots * values.shape[0] * values.shape[1] * width,
            bytes_accessed=6_000_000,
            transcendentals=0,
        ),
    )(*operands)


def gelu_parts(hidden):
    phi = 0.5 + 0.5 * lax.erf(hidden * (0.5**0.5))
    density = jnp.exp(hidden * hidden * -0.5) * 0.3989422804014327
    return hidden * phi, phi + hidden * density


def expert_forward_kernel(
    capacity,
    chunk,
    x_ref,
    cot_ref,
    up_ref,
    bias_up_ref,
    down_ref,
    bias_down_ref,
    result_ref,
    down_grad_ref,
    slope_ref,
    grad_ref,
    bias_grad_ref,
    total_ref,
    grad_t_ref,
    active_ref,
):
    step = pl.program_id(0)
    sources, slots, width = x_ref.shape
    rows = sources * slots
    lanes = round_up(slots, 128)

    @pl.when(step == 0)
    def _():
        bias_grad = jnp.zeros((1, width), F32)
        for s in range(sources):
            parts = x_ref[s, capacity : capacity + 8, :lanes].astype(F32)
            pick = jnp.broadcast_to(parts[0:1] + parts[1:2] + parts[2:3], (128, lanes)).T
            pick = jnp.concatenate([pick[:slots]] * (width // 128), axis=1)
            grad = (pick * cot_ref[s].astype(F32)).astype(BF16)
            grad_ref[s * slots : (s + 1) * slots, :] = grad
            bias_grad = bias_grad + jnp.sum(grad.astype(F32), axis=0, keepdims=True)
        bias_grad_ref[...] = bias_grad
        grad_t_ref[...] = grad_ref[...].T
        total_ref[...] = jnp.broadcast_to(bias_down_ref[...], total_ref.shape)

    x_flat = x_ref.reshape(rows, width)
    for r in range(rows // chunk):
        here = slice(r * chunk, (r + 1) * chunk)
        hidden = dot(x_flat[here, :], up_ref[...]) + bias_up_ref[...]
        active, slope = gelu_parts(hidden)
        active = active.astype(BF16)
        active_ref[here, :] = active
        slope_ref[here, :] = slope.astype(BF16)
        total_ref[here, :] += dot(active, down_ref[...])
    down_grad_ref[0] = dot(grad_t_ref[...], active_ref[...]).astype(BF16)

    @pl.when(step == pl.num_programs(0) - 1)
    def _():
        result_ref[...] = total_ref[...].astype(BF16)


def expert_backward_kernel(
    chunk,
    x_ref,
    grad_ref,
    slope_ref,
    up_ref,
    down_ref,
    entry_ref,
    up_grad_ref,
    bias_grad_ref,
    total_ref,
    x_t_ref,
    hidden_grad_ref,
):
    step = pl.program_id(0)
    rows = grad_ref.shape[0]

    @pl.when(step == 0)
    def _():
        x_t_ref[...] = x_ref[...].T
        total_ref[...] = jnp.zeros_like(total_ref)

    bias_grad = jnp.zeros(bias_grad_ref.shape, F32)
    for r in range(rows // chunk):
        here = slice(r * chunk, (r + 1) * chunk)
        active_grad = dot_nt(grad_ref[here, :], down_ref[...])
        hidden_grad = (active_grad * slope_ref[here, :].astype(F32)).astype(BF16)
        hidden_grad_ref[here, :] = hidden_grad
        bias_grad = bias_grad + jnp.sum(hidden_grad.astype(F32), axis=0, keepdims=True)
        total_ref[here, :] += dot_nt(hidden_grad, up_ref[...])
    bias_grad_ref[...] = bias_grad
    up_grad_ref[...] = dot(x_t_ref[...], hidden_grad_ref[...]).astype(BF16)

    @pl.when(step == pl.num_programs(0) - 1)
    def _():
        entry_ref[...] = total_ref[...].astype(BF16)


def run_experts_forward(x, cot, w_up, b_up, w_down, b_down, capacity, parts):
    sources, slots, width = x.shape
    rows = sources * slots
    units = w_up.shape[1]
    tile = units // parts
    chunk = 512 if rows % 512 == 0 else slots
    return pl.pallas_call(
        functools.partial(expert_forward_kernel, capacity, chunk),
        grid=(parts,),
        in_specs=[
            whole(x.shape),
            whole(cot.shape),
            pl.BlockSpec((width, tile), lambda i: (0, i)),
            pl.BlockSpec((1, tile), lambda i: (0, i)),
            pl.BlockSpec((tile, width), lambda i: (i, 0)),
            whole((1, width)),
        ],
        out_specs=[
            whole((rows, width)),
            pl.BlockSpec((1, width, tile), lambda i: (i, 0, 0)),
            pl.BlockSpec((rows, tile), lambda i: (0, i)),
            whole((rows, width)),
            whole((1, width)),
        ],
        out_shape=[
            jax.ShapeDtypeStruct((rows, width), BF16),
            jax.ShapeDtypeStruct((parts, width, tile), BF16),
            jax.ShapeDtypeStruct((rows, units), BF16),
            jax.ShapeDtypeStruct((rows, width), BF16),
            jax.ShapeDtypeStruct((1, width), F32),
        ],
        scratch_shapes=[
            pltpu.VMEM((rows, width), F32),
            pltpu.VMEM((width, rows), BF16),
            pltpu.VMEM((rows, tile), BF16),
        ],
        compiler_params=params(),
        cost_estimate=pl.CostEstimate(
            flops=6 * rows * width * units, bytes_accessed=40_000_000, transcendentals=rows * units
        ),
    )(x, cot, w_up, b_up, w_down, b_down)


def run_experts_backward(x, grad, slope, w_up, w_down, slots, parts):
    rows, width = x.shape
    units = w_up.shape[1]
    tile = units // parts
    chunk = 512 if rows % 512 == 0 else slots
    return pl.pallas_call(
        functools.partial(expert_backward_kernel, chunk),
        grid=(parts,),
        in_specs=[
            whole(x.shape),
            whole(grad.shape),
            pl.BlockSpec((rows, tile), lambda i: (0, i)),
            pl.BlockSpec((width, tile), lambda i: (0, i)),
            pl.BlockSpec((tile, width), lambda i: (i, 0)),
        ],
        out_specs=[
            whole((rows, width)),
            pl.BlockSpec((width, tile), lambda i: (0, i)),
            pl.BlockSpec((1, tile), lambda i: (0, i)),
        ],
        out_shape=[
            jax.ShapeDtypeStruct((rows, width), BF16),
            jax.ShapeDtypeStruct((width, units), BF16),
            jax.ShapeDtypeStruct((1, units), F32),
        ],
        scratch_shapes=[
            pltpu.VMEM((rows, width), F32),
            pltpu.VMEM((width, rows), BF16),
            pltpu.VMEM((rows, tile), BF16),
        ],
        compiler_params=params(),
        cost_estimate=pl.CostEstimate(
            flops=6 * rows * width * units, bytes_accessed=40_000_000, transcendentals=0
        ),
    )(x, grad, slope, w_up, w_down)


def combine_kernel(
    returned_ref, pos_ref, routes_ref, gates_ref, resid_ref, cot_ref, mixed_ref, logit_grad_ref
):
    slots = returned_ref.shape[0]
    rows, experts = gates_ref.shape[1:]
    gates = gates_ref[0]
    upstream = cot_ref[0].astype(F32)
    slot = lax.broadcasted_iota(jnp.int32, (rows, slots), 1)
    expert = lax.broadcasted_iota(jnp.int32, (rows, experts), 1)
    output = resid_ref[0]
    gate_grad = jnp.zeros((rows, experts), F32)
    for k in range(2):
        hit = jnp.where(pos_ref[0, :, k : k + 1] == slot, 1.0, 0.0).astype(BF16)
        picked = dot(hit, returned_ref[...])
        chosen = routes_ref[0, :, k : k + 1] == expert
        pick = jnp.sum(jnp.where(chosen, gates, 0.0), axis=1, keepdims=True)
        output = output + pick * picked
        pick_grad = jnp.sum(picked * upstream, axis=1, keepdims=True)
        gate_grad = gate_grad + jnp.where(chosen, pick_grad, 0.0)
    mixed_ref[0] = output.astype(BF16)
    logit_grad_ref[0] = gates * (gate_grad - jnp.sum(gates * gate_grad, axis=1, keepdims=True))


def run_combine(returned, pos_cols, routes_cols, gates, resid, cot):
    images, rows, width = resid.shape
    experts = gates.shape[2]
    return pl.pallas_call(
        combine_kernel,
        grid=(images,),
        in_specs=[
            whole(returned.shape),
            per_image(rows, 2),
            per_image(rows, 2),
            per_image(rows, experts),
            per_image(rows, width),
            per_image(rows, width),
        ],
        out_specs=[per_image(rows, width), per_image(rows, experts)],
        out_shape=[
            jax.ShapeDtypeStruct((images, rows, width), BF16),
            jax.ShapeDtypeStruct((images, rows, experts), F32),
        ],
        compiler_params=params(),
        cost_estimate=pl.CostEstimate(
            flops=4 * images * rows * width * returned.shape[0],
            bytes_accessed=10_000_000,
            transcendentals=0,
        ),
    )(returned, pos_cols, routes_cols, gates, resid, cot)


def backward_kernel(
    seq_len,
    entry_ref,
    pos_ref,
    logit_grad_ref,
    low_ref,
    resid_ref,
    cot_ref,
    x_ref,
    q_ref,
    k_ref,
    v_ref,
    att_ref,
    wq_ref,
    wk_ref,
    wv_ref,
    wo_ref,
    vec_ref,
    router_t_ref,
    x_grad_ref,
    first_ref,
    second_ref,
    small_ref,
    router_grad_ref,
    first_sum_ref,
    second_sum_ref,
    dq_ref,
    dk_ref,
    dv_ref,
):
    image = pl.program_id(0)
    slots = entry_ref.shape[0]
    rows, width = low_ref.shape[1:]

    @pl.when(image == 0)
    def _():
        first_sum_ref[...] = jnp.zeros_like(first_sum_ref)
        second_sum_ref[...] = jnp.zeros_like(second_sum_ref)
        small_ref[...] = jnp.zeros_like(small_ref)
        router_grad_ref[...] = jnp.zeros_like(router_grad_ref)

    def add_small(row, values):
        small_ref[row : row + 1, :] += jnp.sum(values, axis=0, keepdims=True)

    slot = lax.broadcasted_iota(jnp.int32, (rows, slots), 1)
    hit = (pos_ref[0, :, 0:1] == slot) | (pos_ref[0, :, 1:2] == slot)
    entry_sum = dot(jnp.where(hit, 1.0, 0.0).astype(BF16), entry_ref[...])
    logit_grad = logit_grad_ref[0]
    low_grad = entry_sum + jnp.dot(logit_grad, router_t_ref[...], precision=HIGHEST)
    router_grad_ref[...] += lax.dot_general(
        logit_grad,
        low_ref[0].astype(F32),
        (((0,), (0,)), ((), ())),
        precision=HIGHEST,
        preferred_element_type=F32,
    )
    unit, inverse = norm_parts(resid_ref[0])
    add_small(5, low_grad * unit)
    add_small(6, low_grad)
    resid_grad = cot_ref[0].astype(F32) + norm_pull(unit, inverse, vec_ref[5:6], low_grad)
    branch_grad = resid_grad.astype(BF16)
    add_small(4, branch_grad.astype(F32))
    second_sum_ref[:, width:] += dot_tn(att_ref[0], branch_grad)
    att_grad = dot_nt(branch_grad, wo_ref[...]).astype(BF16)
    for j in range(HEADS // 2):
        cols = slice(j * PAIR, (j + 1) * PAIR)
        query_stack = stack_heads(q_ref[0, :, cols])
        key_pair = k_ref[0, :, cols]
        probs = pair_probs(query_stack, key_pair, seq_len)
        grad_stack = stack_heads(att_grad[:, cols])
        dv_ref[:, cols] = dot_tn(probs.astype(BF16), grad_stack).astype(BF16)
        probs_grad = dot_nt(grad_stack, v_ref[0, :, cols])
        score_grad = probs * (
            probs_grad - jnp.sum(probs * probs_grad, axis=1, keepdims=True)
        )
        score_grad = score_grad.astype(BF16)
        dq_ref[:, cols] = (merge_heads(dot(score_grad, key_pair)) * SCALE).astype(BF16)
        dk_ref[:, cols] = (dot_tn(score_grad, query_stack) * SCALE).astype(BF16)
    dq, dk, dv = dq_ref[...], dk_ref[...], dv_ref[...]
    add_small(2, dq.astype(F32))
    add_small(3, dv.astype(F32))
    unit, inverse = norm_parts(x_ref[0].astype(F32))
    normed_t = (unit * vec_ref[0:1] + vec_ref[1:2]).astype(BF16).T
    first_sum_ref[:, :width] += dot(normed_t, dq)
    first_sum_ref[:, width:] += dot(normed_t, dk)
    second_sum_ref[:, :width] += dot(normed_t, dv)
    normed_grad = dot_nt(dq, wq_ref[...]) + dot_nt(dk, wk_ref[...]) + dot_nt(dv, wv_ref[...])
    add_small(0, normed_grad * unit)
    add_small(1, normed_grad)
    x_grad_ref[0] = resid_grad + norm_pull(unit, inverse, vec_ref[0:1], normed_grad)

    @pl.when(image == pl.num_programs(0) - 1)
    def _():
        first_ref[...] = first_sum_ref[...].astype(BF16)
        second_ref[...] = second_sum_ref[...].astype(BF16)


def run_backward(
    entry, pos_cols, logit_grad, low, resid, cot, tokens, saved, first, second, vectors, router_t,
    seq_len,
):
    images, rows, width = tokens.shape
    experts = router_t.shape[0]

    def column(j):
        return pl.BlockSpec((width, width), lambda i: (0, j), pipeline_mode=pl.Buffered(1))

    wide = (width, 2 * width)
    return pl.pallas_call(
        functools.partial(backward_kernel, seq_len),
        grid=(images,),
        in_specs=[
            whole(entry.shape),
            per_image(rows, 2),
            per_image(rows, experts),
        ]
        + [per_image(rows, width)] * 8
        + [column(0), column(1), column(0), column(1), whole(vectors.shape), whole(router_t.shape)],
        out_specs=[
            per_image(rows, width),
            whole(wide),
            whole(wide),
            whole((8, width)),
            whole((experts, width)),
        ],
        out_shape=[
            jax.ShapeDtypeStruct((images, rows, width), F32),
            jax.ShapeDtypeStruct(wide, BF16),
            jax.ShapeDtypeStruct(wide, BF16),
            jax.ShapeDtypeStruct((8, width), F32),
            jax.ShapeDtypeStruct((experts, width), F32),
        ],
        scratch_shapes=[pltpu.VMEM(wide, F32), pltpu.VMEM(wide, F32)]
        + [pltpu.VMEM((rows, width), BF16)] * 3,
        compiler_params=params(),
        cost_estimate=pl.CostEstimate(
            flops=24 * images * rows * width * width, bytes_accessed=30_000_000, transcendentals=0
        ),
    )(
        entry, pos_cols, logit_grad, low, resid, cot, tokens, *saved, first, first, second, second,
        vectors, router_t,
    )


def bits_of(size):
    return [1 << i for i in range(size.bit_length() - 1)]


def swap(values, axis, bit):
    return lax.ppermute(values, axis, [(i, i ^ bit) for i in range(lax.axis_size(axis))])


def my_bit(axis, bit):
    return (lax.axis_index(axis) // bit) % 2


def axis_order(reverse):
    expert_bits = bits_of(lax.axis_size("expert"))
    others = expert_bits[1:]
    if not reverse:
        others = others[::-1]
    return [("expert", bit) for bit in others] + [("expert", expert_bits[0])]


def natural_order():
    return [("dp", bit) for bit in bits_of(lax.axis_size("dp"))[::-1]] + [
        ("expert", bit) for bit in bits_of(lax.axis_size("expert"))[::-1]
    ]


def gather_rows(shard, reverse):
    rows, columns = shard.shape
    order = [("dp", bit) for bit in bits_of(lax.axis_size("dp"))] + axis_order(reverse)
    for axis, bit in order:
        other = swap(shard, axis, bit)
        mine_low = my_bit(axis, bit) == 0
        shard = jnp.stack(
            [jnp.where(mine_low, shard, other), jnp.where(mine_low, other, shard)]
        )
    dims = order[::-1]
    turn = [dims.index(pair) for pair in natural_order()]
    shard = shard.transpose(turn + [len(dims), len(dims) + 1])
    return shard.reshape(-1, columns)


def scatter_rows(total, reverse, axes=("dp", "expert")):
    columns = total.shape[-1]
    dims = [pair for pair in natural_order() if pair[0] in axes]
    total = total.reshape((2,) * len(dims) + (-1, columns))
    order = [("dp", bit) for bit in bits_of(lax.axis_size("dp"))] + axis_order(reverse)
    for pair in [p for p in order[::-1] if p[0] in axes]:
        place = dims.index(pair)
        mine = my_bit(*pair)
        sent = lax.dynamic_index_in_dim(total, 1 - mine, place, keepdims=False)
        kept = lax.dynamic_index_in_dim(total, mine, place, keepdims=False)
        total = (kept.astype(F32) + swap(sent, *pair).astype(F32)).astype(total.dtype)
        dims.pop(place)
    return total


def per_device(
    tokens,
    routes,
    gain_one,
    shift_one,
    w_query,
    b_query,
    w_key,
    w_value,
    b_value,
    w_out,
    b_out,
    gain_two,
    shift_two,
    w_router,
    w_up,
    b_up,
    w_down,
    b_down,
    cotangent,
):
    images, seq_len, width = tokens.shape
    token_rows = images * seq_len
    parts = lax.axis_size("dp")
    experts = w_up.shape[0] * lax.axis_size("expert")
    capacity = max((token_rows * 10 // (4 * experts) + 7) // 8 * 8, 8)
    slots = round_up(capacity + 8, 16)
    rows = round_up(seq_len, 16)
    pad = ((0, 0), (0, rows - seq_len), (0, 0))

    vectors = (gain_one, shift_one, b_query, b_value, b_out, gain_two, shift_two)
    spare = jnp.zeros((w_query.shape[0], 128 - len(vectors) - experts), BF16)
    small = jnp.concatenate([jnp.stack(vectors, axis=1), w_router, spare], axis=1)
    first = gather_rows(jnp.concatenate([w_query, w_key], axis=1), False)
    second = gather_rows(jnp.concatenate([w_value, w_out, small], axis=1), True)
    small = second[:, 2 * width :]
    vectors = jnp.pad(small[:, : len(vectors)].T.astype(F32), ((0, 8 - len(vectors)), (0, 0)))
    router = small[:, 7 : 7 + experts]
    router_t = router.T.astype(F32)

    flat_routes = routes.reshape(-1)
    table = (flat_routes[:, None] == jnp.arange(experts, dtype=jnp.int32)[None, :]).astype(
        jnp.int32
    )
    before = jnp.cumsum(table, axis=0) - table
    position = flat_routes * slots + jnp.sum(before * table, axis=1)
    pos_cols = jnp.pad(position.reshape(images, seq_len, 2), pad, constant_values=-1)
    routes_cols = jnp.pad(routes, pad, constant_values=-1)
    pos_rows = pos_cols.transpose(0, 2, 1)

    x = jnp.pad(tokens, pad)
    cot = jnp.pad(cotangent, pad)
    cot_sent = run_dispatch(pos_rows, cot, capacity, slots, experts)
    cot_here = lax.all_to_all(cot_sent, "expert", split_axis=0, concat_axis=0, tiled=True)

    query, key, value, attended, resid, low, gates, gates_t = run_forward(
        x, first, second, vectors, router, seq_len
    )
    low_sent = run_dispatch(pos_rows, low, capacity, slots, experts, gates_t)
    low_here = lax.all_to_all(low_sent, "expert", split_axis=0, concat_axis=0, tiled=True)

    up, down = w_up[0], w_down[0]
    result, down_grad, slope, result_grad, bias_down_grad = run_experts_forward(
        low_here, cot_here, up, b_up.astype(F32), down, b_down.astype(F32), capacity, parts
    )
    returned = lax.all_to_all(
        result.reshape(experts, slots, width), "expert", split_axis=0, concat_axis=0, tiled=True
    )
    down_shard = lax.psum_scatter(down_grad, "dp", scatter_dimension=0, tiled=True)
    entry, up_grad, bias_up_grad = run_experts_backward(
        low_here.reshape(experts * slots, width), result_grad, slope, up, down, slots, parts
    )
    entry_back = lax.all_to_all(
        entry.reshape(experts, slots, width), "expert", split_axis=0, concat_axis=0, tiled=True
    )
    up_shard = lax.psum_scatter(up_grad, "dp", scatter_dimension=0, tiled=True)
    mixed, logit_grad = run_combine(
        returned.reshape(experts * slots, width), pos_cols, routes_cols, gates, resid, cot
    )
    x_grad, first_grad, second_grad, small_grad, router_grad = run_backward(
        entry_back.reshape(experts * slots, width),
        pos_cols,
        logit_grad,
        low,
        resid,
        cot,
        x,
        (query, key, value, attended),
        first,
        second,
        vectors,
        router_t,
        seq_len,
    )
    narrow = jnp.concatenate([small_grad[:7], router_grad], axis=0).T
    narrow = jnp.pad(narrow, ((0, 0), (0, 128 - narrow.shape[1]))).astype(BF16)
    first_shard = scatter_rows(first_grad, False).astype(F32)
    second_shard = scatter_rows(jnp.concatenate([second_grad, narrow], axis=1), True).astype(F32)
    biases = jnp.concatenate(
        [bias_up_grad.reshape(parts, -1), bias_down_grad.reshape(parts, -1)], axis=1
    )
    biases = scatter_rows(biases, False, ("dp",)).reshape(1, -1)
    columns = second_shard[:, 2 * width :]
    tile = down_shard.shape[2]
    return (
        mixed[:, :seq_len],
        x_grad[:, :seq_len],
        columns[:, 0],
        columns[:, 1],
        first_shard[:, :width],
        columns[:, 2],
        first_shard[:, width:],
        second_shard[:, :width],
        columns[:, 3],
        second_shard[:, width : 2 * width],
        columns[:, 4],
        columns[:, 5],
        columns[:, 6],
        columns[:, 7 : 7 + experts],
        up_shard.astype(F32)[None],
        biases[:, :tile],
        down_shard.transpose(0, 2, 1).astype(F32),
        biases[:, tile:],
    )


def solution(mesh):
    both = ("dp", "expert")
    row, matrix, cube = P(both), P(both, None), P(both, None, None)
    return jax.shard_map(
        per_device,
        mesh=mesh,
        in_specs=(
            cube, cube, row, row, matrix, row, matrix, matrix, row, matrix, row, row, row, matrix,
            P("expert", None, None),
            P("expert", None),
            P("expert", None, None),
            P("expert", None),
            cube,
        ),
        out_specs=(
            cube, cube, row, row, matrix, row, matrix, matrix, row, matrix, row, row, row, matrix,
            P("expert", "dp", None),
            P("expert", "dp"),
            P("expert", "dp", None),
            P("expert", "dp"),
        ),
        check_vma=False,
    )
```

```python
import functools

import jax
import jax.numpy as jnp
from jax import lax
from jax.experimental import pallas as pl
from jax.experimental.pallas import tpu as pltpu
from jax.sharding import PartitionSpec as P

HEADS = 12
HEAD_DIM = 64
PAIR = 2 * HEAD_DIM
EPSILON = 1e-06
SCALE = HEAD_DIM**-0.5
HIGHEST = lax.Precision.HIGHEST
VMEM_LIMIT = 60 * 1024 * 1024
BF16 = jnp.bfloat16
F32 = jnp.float32


def round_up(value, unit):
    return -(-value // unit) * unit


def dot(left, right):
    return jnp.dot(left, right, preferred_element_type=F32)


def dot_nt(left, right):
    return lax.dot_general(left, right, (((1,), (1,)), ((), ())), preferred_element_type=F32)


def dot_tn(left, right):
    return lax.dot_general(left, right, (((0,), (0,)), ((), ())), preferred_element_type=F32)


def cost(micros):
    return pl.CostEstimate(
        flops=int(micros * 1.1e9), bytes_accessed=int(micros * 1e6), transcendentals=0
    )


def params(grid_dims=1):
    return pltpu.CompilerParams(
        vmem_limit_bytes=VMEM_LIMIT, dimension_semantics=("arbitrary",) * grid_dims
    )


def whole(shape):
    zeros = (0,) * len(shape)
    return pl.BlockSpec(shape, lambda *_: zeros, pipeline_mode=pl.Buffered(1))


def per_image(*shape):
    zeros = (0,) * len(shape)
    return pl.BlockSpec((1,) + shape, lambda i: (i,) + zeros)


def norm_parts(values):
    center = values - jnp.mean(values, axis=-1, keepdims=True)
    inverse = lax.rsqrt(jnp.mean(center * center, axis=-1, keepdims=True) + EPSILON)
    return center * inverse, inverse


def norm_pull(unit, inverse, gain, grad):
    scaled = grad * gain
    return (
        scaled
        - jnp.mean(scaled, axis=-1, keepdims=True)
        - unit * jnp.mean(scaled * unit, axis=-1, keepdims=True)
    ) * inverse


def stack_heads(pair):
    low_half = lax.broadcasted_iota(jnp.int32, pair.shape, 1) < HEAD_DIM
    zero = jnp.zeros_like(pair)
    return jnp.concatenate(
        [jnp.where(low_half, pair, zero), jnp.where(low_half, zero, pair)], axis=0
    )


def merge_heads(stacked):
    rows = stacked.shape[0] // 2
    low_half = lax.broadcasted_iota(jnp.int32, (rows, PAIR), 1) < HEAD_DIM
    return jnp.where(low_half, stacked[:rows], stacked[rows:])


def pair_probs(query_stack, key_pair, seq_len):
    scores = dot_nt(query_stack, key_pair) * SCALE
    column = lax.broadcasted_iota(jnp.int32, scores.shape, 1)
    scores = jnp.where(column < seq_len, scores, -1e30)
    powers = jnp.exp(scores - jnp.max(scores, axis=1, keepdims=True))
    return powers * (1.0 / jnp.sum(powers, axis=1, keepdims=True))


def forward_kernel(
    seq_len,
    x_ref,
    wq_ref,
    wk_ref,
    wv_ref,
    wo_ref,
    vec_ref,
    router_ref,
    q_ref,
    k_ref,
    v_ref,
    att_ref,
    resid_ref,
    low_ref,
    gates_ref,
    gates_t_ref,
):
    x = x_ref[0].astype(F32)
    unit, _ = norm_parts(x)
    normed = (unit * vec_ref[0:1] + vec_ref[1:2]).astype(BF16)
    q_ref[0] = (dot(normed, wq_ref[...]) + vec_ref[2:3]).astype(BF16)
    k_ref[0] = dot(normed, wk_ref[...]).astype(BF16)
    v_ref[0] = (dot(normed, wv_ref[...]) + vec_ref[3:4]).astype(BF16)
    for j in range(HEADS // 2):
        cols = slice(j * PAIR, (j + 1) * PAIR)
        probs = pair_probs(stack_heads(q_ref[0, :, cols]), k_ref[0, :, cols], seq_len)
        mixed = merge_heads(dot(probs.astype(BF16), v_ref[0, :, cols]))
        att_ref[0, :, cols] = mixed.astype(BF16)
    resid = x + dot(att_ref[0], wo_ref[...]) + vec_ref[4:5]
    resid_ref[0] = resid
    unit_two, _ = norm_parts(resid)
    low = (unit_two * vec_ref[5:6] + vec_ref[6:7]).astype(BF16)
    low_ref[0] = low
    logits = dot(low, router_ref[...])
    powers = jnp.exp(logits - jnp.max(logits, axis=1, keepdims=True))
    gates = powers * (1.0 / jnp.sum(powers, axis=1, keepdims=True))
    gates_ref[0] = gates
    gates_t_ref[0] = gates.T


def run_forward(tokens, dense, vectors, router, seq_len):
    images, rows, width = tokens.shape
    experts = router.shape[1]

    def column(j):
        return pl.BlockSpec((width, width), lambda i: (0, j), pipeline_mode=pl.Buffered(1))

    big = jax.ShapeDtypeStruct((images, rows, width), BF16)
    return pl.pallas_call(
        functools.partial(forward_kernel, seq_len),
        grid=(images,),
        in_specs=[
            per_image(rows, width),
            column(0),
            column(1),
            column(2),
            column(3),
            whole(vectors.shape),
            whole(router.shape),
        ],
        out_specs=[per_image(rows, width)] * 6
        + [per_image(rows, experts), per_image(experts, rows)],
        out_shape=[big, big, big, big, jax.ShapeDtypeStruct(big.shape, F32), big]
        + [
            jax.ShapeDtypeStruct((images, rows, experts), F32),
            jax.ShapeDtypeStruct((images, experts, rows), F32),
        ],
        compiler_params=params(),
        cost_estimate=cost(18),
    )(tokens, dense, dense, dense, dense, vectors, router)


def dispatch_kernel(pos_ref, values_ref, *rest):
    expert = pl.program_id(0)
    images, rows, width = values_ref.shape
    gates_t_ref = rest[0] if len(rest) == 3 else None
    out_refs = rest[-2:] if gates_t_ref is not None else rest
    slots = sum(ref.shape[1] for ref in out_refs)
    half = slots // 2
    lanes = round_up(slots, 128)
    total = jnp.zeros((slots, width), F32)
    parts = jnp.zeros((8, lanes), F32)
    index = lax.broadcasted_iota(jnp.int32, (lanes, rows), 0)
    slot = jnp.where(index < slots, index + expert * slots, -2)
    for b in range(images):
        hit = (pos_ref[b, 0:1] == slot) | (pos_ref[b, 1:2] == slot)
        hit = jnp.where(hit, 1.0, 0.0).astype(BF16)
        total = total + dot(hit[:slots], values_ref[b])
        if gates_t_ref is not None:
            gate = jnp.broadcast_to(gates_t_ref[b, pl.ds(expert, 1)], (8, rows))
            high = gate.astype(BF16).astype(F32)
            middle = (gate - high).astype(BF16).astype(F32)
            part = lax.broadcasted_iota(jnp.int32, gate.shape, 0)
            split = jnp.where(
                part == 0,
                high,
                jnp.where(part == 1, middle, jnp.where(part == 2, gate - high - middle, 0.0)),
            )
            parts = parts + dot_nt(split.astype(BF16), hit)
    if gates_t_ref is None:
        out_refs[0][0] = total.astype(BF16)
        return
    tail = jnp.concatenate([parts, jnp.zeros((8, width - lanes), F32)], axis=1)
    out_refs[0][0] = jnp.concatenate([total[: half - 8], tail], axis=0).astype(BF16)
    out_refs[1][0] = total[half:].astype(BF16)


def run_dispatch(pos_rows, values, slots, experts, gates_t=None):
    width = values.shape[2]
    operands = (pos_rows, values) + (() if gates_t is None else (gates_t,))
    pieces = [slots] if gates_t is None else [slots // 2] * 2
    return pl.pallas_call(
        dispatch_kernel,
        grid=(experts,),
        in_specs=[whole(o.shape) for o in operands],
        out_specs=[pl.BlockSpec((1, piece, width), lambda i: (i, 0, 0)) for piece in pieces],
        out_shape=[jax.ShapeDtypeStruct((experts, piece, width), BF16) for piece in pieces],
        compiler_params=params(),
        cost_estimate=cost(7.5),
    )(*operands)


def gelu_parts(hidden):
    phi = 0.5 + 0.5 * lax.erf(hidden * (0.5**0.5))
    density = jnp.exp(hidden * hidden * -0.5) * 0.3989422804014327
    return hidden * phi, phi + hidden * density


def expert_forward_kernel(
    part,
    chunk,
    x_ref,
    cot_ref,
    picks_ref,
    up_ref,
    bias_up_ref,
    down_ref,
    bias_down_ref,
    *rest,
):
    carry_ref, before_ref = rest[:2] if len(rest) == 10 else (None, None)
    (
        result_ref,
        down_grad_ref,
        slope_ref,
        grad_ref,
        bias_grad_ref,
        total_ref,
        grad_t_ref,
        active_ref,
    ) = rest[-8:]
    step = pl.program_id(0)
    sources, slots, width = x_ref.shape
    rows = sources * slots
    lanes = picks_ref.shape[2]

    @pl.when(step == 0)
    def _():
        bias_grad = jnp.zeros((1, width), F32)
        for s in range(sources):
            parts = picks_ref[s].astype(F32)
            pick = jnp.broadcast_to(parts[0:1] + parts[1:2] + parts[2:3], (128, lanes)).T
            pick = pick[part * slots : (part + 1) * slots]
            pick = jnp.concatenate([pick] * (width // 128), axis=1)
            grad = (pick * cot_ref[s].astype(F32)).astype(BF16)
            grad_ref[s * slots : (s + 1) * slots, :] = grad
            bias_grad = bias_grad + jnp.sum(grad.astype(F32), axis=0, keepdims=True)
        bias_grad_ref[...] = bias_grad
        grad_t_ref[...] = grad_ref[...].T
        total_ref[...] = jnp.broadcast_to(bias_down_ref[...], total_ref.shape)

    x_flat = x_ref.reshape(rows, width)
    for r in range(rows // chunk):
        here = slice(r * chunk, (r + 1) * chunk)
        hidden = dot(x_flat[here, :], up_ref[...]) + bias_up_ref[...]
        active, slope = gelu_parts(hidden)
        active = active.astype(BF16)
        active_ref[here, :] = active
        slope_ref[here, :] = slope.astype(BF16)
        total_ref[here, :] += dot(active, down_ref[...])
    down_grad = dot(grad_t_ref[...], active_ref[...])
    if carry_ref is not None:
        down_grad = down_grad + carry_ref[0]
    down_grad_ref[0] = down_grad.astype(down_grad_ref.dtype)

    @pl.when(step == pl.num_programs(0) - 1)
    def _():
        result = total_ref[...].astype(BF16)
        if before_ref is None:
            result_ref[...] = result
            return
        for s in range(sources):
            here = slice(s * slots, (s + 1) * slots)
            result_ref[s, :slots] = before_ref[here, :]
            result_ref[s, slots:] = result[here]


def expert_backward_kernel(
    chunk,
    x_ref,
    x_more_ref,
    grad_ref,
    grad_more_ref,
    slope_ref,
    slope_more_ref,
    up_ref,
    down_ref,
    entry_ref,
    up_grad_ref,
    bias_grad_ref,
    total_ref,
    x_t_ref,
    hidden_grad_ref,
):
    step = pl.program_id(0)
    rows = grad_ref.shape[0]
    sources, slots, _ = entry_ref.shape
    half = slots // 2

    @pl.when(step == 0)
    def _():
        x_t_ref[:, :rows] = x_ref[...].T
        x_t_ref[:, rows:] = x_more_ref[...].T
        total_ref[...] = jnp.zeros_like(total_ref)

    bias_grad = jnp.zeros(bias_grad_ref.shape, F32)
    for part, (grads, slopes) in enumerate(((grad_ref, slope_ref), (grad_more_ref, slope_more_ref))):
        for r in range(rows // chunk):
            here = slice(r * chunk, (r + 1) * chunk)
            there = slice(part * rows + r * chunk, part * rows + (r + 1) * chunk)
            active_grad = dot_nt(grads[here, :], down_ref[...])
            hidden_grad = (active_grad * slopes[here, :].astype(F32)).astype(BF16)
            hidden_grad_ref[there, :] = hidden_grad
            bias_grad = bias_grad + jnp.sum(hidden_grad.astype(F32), axis=0, keepdims=True)
            total_ref[there, :] += dot_nt(hidden_grad, up_ref[...])
    bias_grad_ref[...] = bias_grad
    up_grad_ref[...] = dot(x_t_ref[...], hidden_grad_ref[...]).astype(BF16)

    @pl.when(step == pl.num_programs(0) - 1)
    def _():
        for part in range(2):
            for s in range(sources):
                place = part * rows + s * half
                entry_ref[s, part * half : (part + 1) * half] = total_ref[
                    place : place + half, :
                ].astype(BF16)


def chunk_of(rows):
    for size in (512, 256, 128, 64, 32):
        if rows % size == 0:
            return size
    return rows


def run_experts_forward(part, x, cot, picks, w_up, b_up, w_down, b_down, parts, earlier=None):
    sources, slots, width = x.shape
    rows = sources * slots
    result_shape = (rows, width) if earlier is None else (sources, 2 * slots, width)
    units = w_up.shape[1]
    tile = units // parts
    carried = pl.BlockSpec((1, width, tile), lambda i: (i, 0, 0))
    return pl.pallas_call(
        functools.partial(expert_forward_kernel, part, chunk_of(rows)),
        grid=(parts,),
        in_specs=[
            whole(x.shape),
            pl.BlockSpec(x.shape, lambda i: (0, part, 0), pipeline_mode=pl.Buffered(1)),
            whole(picks.shape),
            pl.BlockSpec((width, tile), lambda i: (0, i)),
            pl.BlockSpec((1, tile), lambda i: (0, i)),
            pl.BlockSpec((tile, width), lambda i: (i, 0)),
            whole((1, width)),
        ]
        + ([] if earlier is None else [carried, whole((rows, width))]),
        out_specs=[
            whole(result_shape),
            carried,
            pl.BlockSpec((rows, tile), lambda i: (0, i)),
            whole((rows, width)),
            whole((1, width)),
        ],
        out_shape=[
            jax.ShapeDtypeStruct(result_shape, BF16),
            jax.ShapeDtypeStruct((parts, width, tile), F32 if earlier is None else BF16),
            jax.ShapeDtypeStruct((rows, units), BF16),
            jax.ShapeDtypeStruct((rows, width), BF16),
            jax.ShapeDtypeStruct((1, width), F32),
        ],
        scratch_shapes=[
            pltpu.VMEM((rows, width), F32),
            pltpu.VMEM((width, rows), BF16),
            pltpu.VMEM((rows, tile), BF16),
        ],
        compiler_params=params(),
        cost_estimate=cost(24),
    )(x, cot, picks, w_up, b_up, w_down, b_down, *(() if earlier is None else earlier))


def run_experts_backward(x, grad, slope, w_up, w_down, sources, parts):
    rows, width = x[0].shape
    units = w_up.shape[1]
    tile = units // parts
    entry_shape = (sources, 2 * rows // sources, width)
    return pl.pallas_call(
        functools.partial(expert_backward_kernel, chunk_of(rows)),
        grid=(parts,),
        in_specs=[whole((rows, width))] * 4
        + [pl.BlockSpec((rows, tile), lambda i: (0, i))] * 2
        + [
            pl.BlockSpec((width, tile), lambda i: (0, i)),
            pl.BlockSpec((tile, width), lambda i: (i, 0)),
        ],
        out_specs=[
            whole(entry_shape),
            pl.BlockSpec((width, tile), lambda i: (0, i)),
            pl.BlockSpec((1, tile), lambda i: (0, i)),
        ],
        out_shape=[
            jax.ShapeDtypeStruct(entry_shape, BF16),
            jax.ShapeDtypeStruct((width, units), BF16),
            jax.ShapeDtypeStruct((1, units), F32),
        ],
        scratch_shapes=[
            pltpu.VMEM((2 * rows, width), F32),
            pltpu.VMEM((width, 2 * rows), BF16),
            pltpu.VMEM((2 * rows, tile), BF16),
        ],
        compiler_params=params(),
        cost_estimate=cost(40),
    )(*x, *grad, *slope, w_up, w_down)


def gather_slots(places, values_ref):
    slot = lax.broadcasted_iota(jnp.int32, (places[0].shape[0], values_ref.shape[0]), 1)
    hit = places[0] == slot
    for place in places[1:]:
        hit = hit | (place == slot)
    return dot(jnp.where(hit, 1.0, 0.0).astype(BF16), values_ref[...])


def combine_kernel(
    seq_len,
    returned_ref,
    pos_ref,
    routes_ref,
    gates_ref,
    resid_ref,
    cot_ref,
    low_ref,
    x_ref,
    q_ref,
    k_ref,
    att_ref,
    vec_ref,
    router_t_ref,
    mixed_ref,
    low_grad_ref,
    router_grad_ref,
    probs_ref,
    probs_t_ref,
    normed_t_ref,
    att_t_ref,
):
    rows, experts = gates_ref.shape[1:]

    @pl.when(pl.program_id(0) == 0)
    def _():
        router_grad_ref[...] = jnp.zeros_like(router_grad_ref)

    for j in range(HEADS // 2):
        cols = slice(j * PAIR, (j + 1) * PAIR)
        probs = pair_probs(stack_heads(q_ref[0, :, cols]), k_ref[0, :, cols], seq_len)
        probs_ref[0, j] = probs
        probs_t_ref[0, j] = probs.astype(BF16).T
    unit, _ = norm_parts(x_ref[0].astype(F32))
    normed_t_ref[0] = (unit * vec_ref[0:1] + vec_ref[1:2]).astype(BF16).T
    att_t_ref[0] = att_ref[0].T

    gates = gates_ref[0]
    upstream = cot_ref[0].astype(F32)
    expert = lax.broadcasted_iota(jnp.int32, (rows, experts), 1)
    output = resid_ref[0]
    gate_grad = jnp.zeros((rows, experts), F32)
    for k in range(2):
        picked = gather_slots([pos_ref[0, :, k : k + 1]], returned_ref)
        chosen = routes_ref[0, :, k : k + 1] == expert
        pick = jnp.sum(jnp.where(chosen, gates, 0.0), axis=1, keepdims=True)
        output = output + pick * picked
        pick_grad = jnp.sum(picked * upstream, axis=1, keepdims=True)
        gate_grad = gate_grad + jnp.where(chosen, pick_grad, 0.0)
    mixed_ref[0] = output.astype(BF16)[:seq_len]
    logit_grad = gates * (gate_grad - jnp.sum(gates * gate_grad, axis=1, keepdims=True))
    low_grad_ref[0] = jnp.dot(logit_grad, router_t_ref[...], precision=HIGHEST)
    router_grad_ref[...] += lax.dot_general(
        logit_grad,
        low_ref[0].astype(F32),
        (((0,), (0,)), ((), ())),
        precision=HIGHEST,
        preferred_element_type=F32,
    )


def run_combine(
    returned, pos_cols, routes_cols, gates, resid, cot, low, x, query, key,
    attended, vectors, router_t, seq_len,
):
    images, rows, width = resid.shape
    experts = gates.shape[2]
    pairs = HEADS // 2
    return pl.pallas_call(
        functools.partial(combine_kernel, seq_len),
        grid=(images,),
        in_specs=[
            whole(returned.shape),
            per_image(rows, 2),
            per_image(rows, 2),
            per_image(rows, experts),
        ]
        + [per_image(rows, width)] * 7
        + [whole(vectors.shape), whole(router_t.shape)],
        out_specs=[
            per_image(seq_len, width),
            per_image(rows, width),
            whole((experts, width)),
            per_image(pairs, 2 * rows, rows),
            per_image(pairs, rows, 2 * rows),
            per_image(width, rows),
            per_image(width, rows),
        ],
        out_shape=[
            jax.ShapeDtypeStruct((images, seq_len, width), BF16),
            jax.ShapeDtypeStruct((images, rows, width), F32),
            jax.ShapeDtypeStruct((experts, width), F32),
            jax.ShapeDtypeStruct((images, pairs, 2 * rows, rows), F32),
            jax.ShapeDtypeStruct((images, pairs, rows, 2 * rows), BF16),
            jax.ShapeDtypeStruct((images, width, rows), BF16),
            jax.ShapeDtypeStruct((images, width, rows), BF16),
        ],
        compiler_params=params(),
        cost_estimate=cost(20),
    )(
        returned, pos_cols, routes_cols, gates, resid, cot, low, x, query, key,
        attended, vectors, router_t,
    )


def branch_kernel(
    entry_ref,
    pos_ref,
    low_grad_ref,
    resid_ref,
    cot_ref,
    probs_ref,
    probs_t_ref,
    q_ref,
    k_ref,
    v_ref,
    normed_t_ref,
    att_t_ref,
    wo_ref,
    wq_ref,
    wk_ref,
    wv_ref,
    columns_ref,
    vec_ref,
    router_grad_ref,
    resid_grad_ref,
    dq_ref,
    dk_ref,
    dv_ref,
    first_ref,
    second_ref,
    first_sum_ref,
    second_sum_ref,
    small_ref,
):
    image = pl.program_id(0)
    rows, width = resid_ref.shape[1:]

    @pl.when(image == 0)
    def _():
        first_sum_ref[...] = jnp.zeros_like(first_sum_ref)
        second_sum_ref[...] = jnp.zeros_like(second_sum_ref)
        small_ref[...] = jnp.zeros_like(small_ref)

    def add_small(row, values):
        small_ref[row : row + 1, :] += jnp.sum(values, axis=0, keepdims=True)

    low_grad = low_grad_ref[0] + gather_slots(
        [pos_ref[0, :, 0:1], pos_ref[0, :, 1:2]], entry_ref
    )
    unit, inverse = norm_parts(resid_ref[0])
    add_small(5, low_grad * unit)
    add_small(6, low_grad)
    resid_grad = cot_ref[0].astype(F32) + norm_pull(unit, inverse, vec_ref[5:6], low_grad)
    resid_grad_ref[0] = resid_grad
    branch_grad = resid_grad.astype(BF16)
    add_small(4, branch_grad.astype(F32))
    second_sum_ref[:, width:] += dot(att_t_ref[0], branch_grad)
    att_grad = dot_nt(branch_grad, wo_ref[...]).astype(BF16)
    for j in range(HEADS // 2):
        cols = slice(j * PAIR, (j + 1) * PAIR)
        query_stack = stack_heads(q_ref[0, :, cols])
        key_pair = k_ref[0, :, cols]
        probs = probs_ref[0, j]
        grad_stack = stack_heads(att_grad[:, cols])
        dv_ref[0, :, cols] = dot(probs_t_ref[0, j], grad_stack).astype(BF16)
        probs_grad = dot_nt(grad_stack, v_ref[0, :, cols])
        score_grad = probs * (
            probs_grad - jnp.sum(probs * probs_grad, axis=1, keepdims=True)
        )
        score_grad = score_grad.astype(BF16)
        dq_ref[0, :, cols] = (merge_heads(dot(score_grad, key_pair)) * SCALE).astype(BF16)
        dk_ref[0, :, cols] = (dot_tn(score_grad, query_stack) * SCALE).astype(BF16)
    dq, dk, dv = dq_ref[0], dk_ref[0], dv_ref[0]
    add_small(2, dq.astype(F32))
    add_small(3, dv.astype(F32))
    add_small(7, dk.astype(F32))
    normed_t = normed_t_ref[0]
    first_sum_ref[:, :width] += dot(normed_t, dq)
    first_sum_ref[:, width:] += dot(normed_t, dk)
    second_sum_ref[:, :width] += dot(normed_t, dv)

    @pl.when(image == pl.num_programs(0) - 1)
    def _():
        first_ref[...] = first_sum_ref[...].astype(BF16)
        second_ref[:, : 2 * width] = second_sum_ref[...].astype(BF16)
        gain = 1.0 / columns_ref[:, 0:1].astype(F32)
        shift = columns_ref[:, 1:2].astype(F32)
        gain_grad = jnp.zeros((width, 1), F32)
        shift_grad = jnp.zeros((width, 1), F32)
        for weight_ref, sum_ref, start, row in (
            (wq_ref, first_sum_ref, 0, 2),
            (wk_ref, first_sum_ref, width, 7),
            (wv_ref, second_sum_ref, 0, 3),
        ):
            weight = weight_ref[...].astype(F32)
            bias = small_ref[row : row + 1, :]
            scaled = sum_ref[:, start : start + width] - shift * bias
            gain_grad = gain_grad + jnp.sum(weight * scaled, axis=1, keepdims=True)
            shift_grad = shift_grad + jnp.sum(weight * bias, axis=1, keepdims=True)
        narrow = jnp.concatenate([small_ref[...], router_grad_ref[...]], axis=0)
        narrow = jnp.concatenate(
            [narrow, jnp.zeros((128 - narrow.shape[0], width), F32)], axis=0
        ).T
        lane = lax.broadcasted_iota(jnp.int32, narrow.shape, 1)
        narrow = jnp.where(lane == 0, gain_grad * gain, jnp.where(lane == 1, shift_grad, narrow))
        second_ref[:, 2 * width :] = narrow.astype(BF16)


def run_branch(
    entry, pos_cols, low_grad, resid, cot, probs, probs_t, query, key, value,
    normed_t, att_t, dense, vectors, router_grad,
):
    images, rows, width = resid.shape
    pairs = HEADS // 2
    wide = (width, 2 * width)
    wider = (width, 2 * width + 128)

    def column(j):
        return pl.BlockSpec((width, width), lambda i: (0, j), pipeline_mode=pl.Buffered(1))

    low_shape = jax.ShapeDtypeStruct((images, rows, width), BF16)
    return pl.pallas_call(
        branch_kernel,
        grid=(images,),
        in_specs=[whole(entry.shape), per_image(rows, 2)]
        + [per_image(rows, width)] * 3
        + [per_image(pairs, 2 * rows, rows), per_image(pairs, rows, 2 * rows)]
        + [per_image(rows, width)] * 3
        + [per_image(width, rows)] * 2
        + [
            column(3),
            column(0),
            column(1),
            column(2),
            pl.BlockSpec(
                (width, 128), lambda i: (0, 4 * width // 128), pipeline_mode=pl.Buffered(1)
            ),
            whole(vectors.shape),
            whole(router_grad.shape),
        ],
        out_specs=[per_image(rows, width)] * 4 + [whole(wide), whole(wider)],
        out_shape=[
            jax.ShapeDtypeStruct((images, rows, width), F32),
            low_shape,
            low_shape,
            low_shape,
            jax.ShapeDtypeStruct(wide, BF16),
            jax.ShapeDtypeStruct(wider, BF16),
        ],
        scratch_shapes=[
            pltpu.VMEM(wide, F32),
            pltpu.VMEM(wide, F32),
            pltpu.VMEM((8, width), F32),
        ],
        compiler_params=params(),
        cost_estimate=cost(36),
    )(
        entry, pos_cols, low_grad, resid, cot, probs, probs_t, query, key, value,
        normed_t, att_t, dense, dense, dense, dense, dense, vectors, router_grad,
    )


def input_kernel(
    dq_ref, dk_ref, dv_ref, wq_ref, wk_ref, wv_ref, x_ref, resid_grad_ref, vec_ref, x_grad_ref
):
    seq_len = x_grad_ref.shape[1]
    unit, inverse = norm_parts(x_ref[0].astype(F32))
    normed_grad = (
        dot_nt(dq_ref[0], wq_ref[...])
        + dot_nt(dk_ref[0], wk_ref[...])
        + dot_nt(dv_ref[0], wv_ref[...])
    )
    x_grad = resid_grad_ref[0] + norm_pull(unit, inverse, vec_ref[0:1], normed_grad)
    x_grad_ref[0] = x_grad[:seq_len]


def run_input(dq, dk, dv, dense, x, resid_grad, vectors, seq_len):
    images, rows, width = x.shape

    def column(j):
        return pl.BlockSpec((width, width), lambda i: (0, j), pipeline_mode=pl.Buffered(1))

    return pl.pallas_call(
        input_kernel,
        grid=(images,),
        in_specs=[per_image(rows, width)] * 3
        + [column(0), column(1), column(2)]
        + [per_image(rows, width)] * 2
        + [whole(vectors.shape)],
        out_specs=per_image(seq_len, width),
        out_shape=jax.ShapeDtypeStruct((images, seq_len, width), F32),
        compiler_params=params(),
        cost_estimate=cost(10),
    )(dq, dk, dv, dense, dense, dense, x, resid_grad, vectors)


def bits_of(size):
    return [1 << i for i in range(size.bit_length() - 1)]


def swap(values, axis, bit):
    return lax.ppermute(values, axis, [(i, i ^ bit) for i in range(lax.axis_size(axis))])


def my_bit(axis, bit):
    return (lax.axis_index(axis) // bit) % 2


def plane_bits():
    return bits_of(lax.axis_size("expert"))[1:]


def expert_bits():
    return bits_of(lax.axis_size("expert"))[::-1]


def gather_line(shard, axis):
    count, me = lax.axis_size(axis), lax.axis_index(axis)
    got = [
        lax.ppermute(shard, axis, [(i, (i + k) % count) for i in range(count)])
        for k in range(count - 1, 0, -1)
    ]
    ring = jnp.stack((got + [shard]) * 2)
    return lax.dynamic_slice_in_dim(ring, count - 1 - me, count, 0)


def gather_plane(shard):
    chips = lax.axis_size("expert") // 2
    got = [shard] + [swap(shard, "expert", 2 * k) for k in range(1, chips)]
    out = jnp.stack(got, axis=1)
    for bit in bits_of(chips):
        cut = out.reshape((out.shape[0], chips // (2 * bit), 2, bit) + out.shape[2:])
        turned = jnp.where(my_bit("expert", 2 * bit) == 1, cut[:, :, ::-1], cut)
        out = turned.reshape(out.shape)
    return out


def gather_core(shard):
    other = swap(shard, "expert", 1)
    mine_low = my_bit("expert", 1) == 0
    both = jnp.stack(
        [jnp.where(mine_low, shard, other), jnp.where(mine_low, other, shard)], axis=2
    )
    return both.reshape(-1, shard.shape[-1])


def scatter_line(total, axis):
    count, me = lax.axis_size(axis), lax.axis_index(axis)
    kept = lax.dynamic_index_in_dim(total, me, 0, keepdims=False).astype(F32)
    for k in range(1, count):
        sent = lax.dynamic_index_in_dim(total, (me + k) % count, 0, keepdims=False)
        got = lax.ppermute(sent, axis, [(i, (i + k) % count) for i in range(count)])
        kept = kept + got.astype(F32)
    return kept


def scatter_start(total):
    dims = expert_bits()
    return total.reshape((lax.axis_size("dp"),) + (2,) * len(dims) + (-1, total.shape[-1])), dims


def scatter_bits(state, bits):
    total, dims = state
    dims = list(dims)
    for bit in bits:
        place = dims.index(bit) + 1
        mine = my_bit("expert", bit)
        sent = lax.dynamic_index_in_dim(total, 1 - mine, place, keepdims=False)
        kept = lax.dynamic_index_in_dim(total, mine, place, keepdims=False)
        total = (kept.astype(F32) + swap(sent, "expert", bit).astype(F32)).astype(total.dtype)
        dims.remove(bit)
    return total, dims


def exchange(values):
    return lax.all_to_all(values, "expert", split_axis=0, concat_axis=0, tiled=True)


def exchange_after(values, earlier):
    if earlier is not None:
        values, _ = lax.optimization_barrier((values, earlier))
    return exchange(values)


def per_device(
    tokens,
    routes,
    gain_one,
    shift_one,
    w_query,
    b_query,
    w_key,
    w_value,
    b_value,
    w_out,
    b_out,
    gain_two,
    shift_two,
    w_router,
    w_up,
    b_up,
    w_down,
    b_down,
    cotangent,
):
    images, seq_len, width = tokens.shape
    token_rows = images * seq_len
    parts = lax.axis_size("dp")
    experts = w_up.shape[0] * lax.axis_size("expert")
    capacity = max((token_rows * 10 // (4 * experts) + 7) // 8 * 8, 8)
    slots = round_up(capacity + 8, 32)
    half = slots // 2
    lanes = round_up(slots, 128)
    rows = round_up(seq_len, 16)
    pad = ((0, 0), (0, rows - seq_len), (0, 0))

    vectors = (gain_one, shift_one, b_query, b_value, b_out, gain_two, shift_two)
    spare = jnp.zeros((w_query.shape[0], 128 - len(vectors) - experts), BF16)
    small = jnp.concatenate([jnp.stack(vectors, axis=1), w_router, spare], axis=1)
    shard = jnp.concatenate([w_query, w_key, w_value, w_out, small], axis=1)
    shard = gather_line(shard, "dp")

    flat_routes = routes.reshape(-1)
    table = (flat_routes[:, None] == jnp.arange(experts, dtype=jnp.int32)[None, :]).astype(
        jnp.int32
    )
    before = jnp.cumsum(table, axis=0) - table
    slot = jnp.sum(before * table, axis=1)
    slot = jnp.where(slot < half - 8, slot, slot + 8)
    pos_cols = (flat_routes * slots + slot).reshape(images, seq_len, 2)
    pos_cols = jnp.pad(pos_cols, pad, constant_values=-1)
    pos_rows = pos_cols.transpose(0, 2, 1)
    routes_cols = jnp.pad(routes, pad, constant_values=-1)

    x = jnp.pad(tokens, pad)
    cot = jnp.pad(cotangent, pad)
    shard, pos_sent, x = lax.optimization_barrier((shard, pos_rows, x))
    shard = gather_plane(shard)
    (cot_sent,) = run_dispatch(pos_sent, cot, slots, experts)
    shard, cot_sent, x = lax.optimization_barrier((shard, cot_sent, x))
    cot_here = exchange(cot_sent)
    dense = gather_core(shard)
    small = dense[:, 4 * width :]
    vectors = jnp.pad(small[:, : len(vectors)].T.astype(F32), ((0, 8 - len(vectors)), (0, 0)))
    router = small[:, 7 : 7 + experts]
    router_t = router.T.astype(F32)

    query, key, value, attended, resid, low, gates, gates_t = run_forward(
        x, dense, vectors, router, seq_len
    )
    up, down = w_up[0], w_down[0]
    bias_up, bias_down = b_up.astype(F32), b_down.astype(F32)
    low_sent = run_dispatch(pos_rows, low, slots, experts, gates_t)
    low_here, sent = [], cot_here
    for piece in low_sent:
        sent = exchange_after(piece, sent)
        low_here.append(sent)
    picks = low_here[0][:, half - 8 :, :lanes]
    forward, earlier = [], None
    for i in range(2):
        step = run_experts_forward(
            i, low_here[i], cot_here, picks, up, bias_up, down, bias_down, parts, earlier
        )
        earlier = (step[1], step[0])
        forward.append(step)
    result, down_grad = forward[1][:2]
    returned = exchange_after(result, sent)
    down_shard = lax.psum_scatter(down_grad, "dp", scatter_dimension=0, tiled=True)
    entry, up_grad, bias_up_grad = run_experts_backward(
        [piece.reshape(-1, width) for piece in low_here],
        [step[3] for step in forward],
        [step[2] for step in forward],
        up,
        down,
        experts,
        parts,
    )
    entry_back = exchange_after(entry, returned)
    up_shard = lax.psum_scatter(up_grad, "dp", scatter_dimension=0, tiled=True)
    bias_down_grad = forward[0][4] + forward[1][4]
    biases = jnp.concatenate(
        [bias_up_grad.reshape(parts, -1), bias_down_grad.reshape(parts, -1)], axis=1
    )
    biases = scatter_line(biases, "dp")[None]
    mixed, low_grad, router_grad, probs, probs_t, normed_t, att_t = run_combine(
        returned.reshape(-1, width),
        pos_cols,
        routes_cols,
        gates,
        resid,
        cot,
        low,
        x,
        query,
        key,
        attended,
        vectors,
        router_t,
        seq_len,
    )
    entry_back, biases = lax.optimization_barrier((entry_back, biases))
    resid_grad, dq, dk, dv, first_grad, second_grad = run_branch(
        entry_back.reshape(-1, width),
        pos_cols,
        low_grad,
        resid,
        cot,
        probs,
        probs_t,
        query,
        key,
        value,
        normed_t,
        att_t,
        dense,
        vectors,
        router_grad,
    )
    others = plane_bits()
    down_shard = down_shard.transpose(0, 2, 1).astype(F32)
    first_grad = scatter_bits(scatter_start(first_grad), [1])
    second_grad = scatter_bits(scatter_start(second_grad), [1])
    first_part, second_part, dv, down_shard = lax.optimization_barrier(
        (first_grad[0], second_grad[0], dv, down_shard)
    )
    first_grad = scatter_bits((first_part, first_grad[1]), others[-1:])
    second_grad = scatter_bits((second_part, second_grad[1]), others[:1])
    x_grad = run_input(dq, dk, dv, dense, x, resid_grad, vectors, seq_len)
    first_part, second_part, x_grad = lax.optimization_barrier(
        (first_grad[0], second_grad[0], x_grad)
    )
    first_grad = scatter_bits((first_part, first_grad[1]), others[:-1][::-1])
    second_grad = scatter_bits((second_part, second_grad[1]), others[1:])
    first_shard = scatter_line(first_grad[0], "dp")
    second_shard = scatter_line(second_grad[0], "dp")
    up_shard, first_shard, second_shard = lax.optimization_barrier(
        (up_shard, first_shard, second_shard)
    )
    columns = second_shard[:, 2 * width :]
    tile = down_shard.shape[1]
    return (
        mixed,
        x_grad,
        columns[:, 0],
        columns[:, 1],
        first_shard[:, :width],
        columns[:, 2],
        first_shard[:, width:],
        second_shard[:, :width],
        columns[:, 3],
        second_shard[:, width : 2 * width],
        columns[:, 4],
        columns[:, 5],
        columns[:, 6],
        columns[:, 8 : 8 + experts],
        up_shard.astype(F32)[None],
        biases[:, :tile],
        down_shard,
        biases[:, tile:],
    )


def solution(mesh):
    both = ("dp", "expert")
    row, matrix, cube = P(both), P(both, None), P(both, None, None)
    return jax.shard_map(
        per_device,
        mesh=mesh,
        in_specs=(
            cube, cube, row, row, matrix, row, matrix, matrix, row, matrix, row, row, row, matrix,
            P("expert", None, None),
            P("expert", None),
            P("expert", None, None),
            P("expert", None),
            cube,
        ),
        out_specs=(
            cube, cube, row, row, matrix, row, matrix, matrix, row, matrix, row, row, row, matrix,
            P("expert", "dp", None),
            P("expert", "dp"),
            P("expert", "dp", None),
            P("expert", "dp"),
        ),
        check_vma=False,
    )
```

```python
import functools

import jax
import jax.numpy as jnp
from jax import lax
from jax.experimental import pallas as pl
from jax.experimental.pallas import tpu as pltpu
from jax.sharding import PartitionSpec as P

HEADS = 12
HEAD_DIM = 64
PAIR = 2 * HEAD_DIM
EPSILON = 1e-06
SCALE = HEAD_DIM**-0.5
HIGHEST = lax.Precision.HIGHEST
VMEM_LIMIT = 60 * 1024 * 1024
BF16 = jnp.bfloat16
F32 = jnp.float32


def round_up(value, unit):
    return -(-value // unit) * unit


def dot(left, right):
    return jnp.dot(left, right, preferred_element_type=F32)


def dot_nt(left, right):
    return lax.dot_general(left, right, (((1,), (1,)), ((), ())), preferred_element_type=F32)


def dot_tn(left, right):
    return lax.dot_general(left, right, (((0,), (0,)), ((), ())), preferred_element_type=F32)


def cost(micros):
    return pl.CostEstimate(
        flops=int(micros * 1.1e9), bytes_accessed=int(micros * 1e6), transcendentals=0
    )


def params(grid_dims=1):
    return pltpu.CompilerParams(
        vmem_limit_bytes=VMEM_LIMIT, dimension_semantics=("arbitrary",) * grid_dims
    )


def whole(shape):
    zeros = (0,) * len(shape)
    return pl.BlockSpec(shape, lambda *_: zeros, pipeline_mode=pl.Buffered(1))


def per_image(*shape):
    zeros = (0,) * len(shape)
    return pl.BlockSpec((1,) + shape, lambda i: (i,) + zeros)


def norm_parts(values):
    center = values - jnp.mean(values, axis=-1, keepdims=True)
    inverse = lax.rsqrt(jnp.mean(center * center, axis=-1, keepdims=True) + EPSILON)
    return center * inverse, inverse


def norm_pull(unit, inverse, gain, grad):
    scaled = grad * gain
    return (
        scaled
        - jnp.mean(scaled, axis=-1, keepdims=True)
        - unit * jnp.mean(scaled * unit, axis=-1, keepdims=True)
    ) * inverse


def stack_heads(pair):
    low_half = lax.broadcasted_iota(jnp.int32, pair.shape, 1) < HEAD_DIM
    zero = jnp.zeros_like(pair)
    return jnp.concatenate(
        [jnp.where(low_half, pair, zero), jnp.where(low_half, zero, pair)], axis=0
    )


def merge_heads(stacked):
    rows = stacked.shape[0] // 2
    low_half = lax.broadcasted_iota(jnp.int32, (rows, PAIR), 1) < HEAD_DIM
    return jnp.where(low_half, stacked[:rows], stacked[rows:])


def pair_probs(query_stack, key_pair, seq_len):
    scores = dot_nt(query_stack, key_pair) * SCALE
    column = lax.broadcasted_iota(jnp.int32, scores.shape, 1)
    scores = jnp.where(column < seq_len, scores, -1e30)
    powers = jnp.exp(scores - jnp.max(scores, axis=1, keepdims=True))
    return powers * (1.0 / jnp.sum(powers, axis=1, keepdims=True))


def forward_kernel(
    seq_len,
    x_ref,
    wq_ref,
    wk_ref,
    wv_ref,
    wo_ref,
    vec_ref,
    router_ref,
    q_ref,
    k_ref,
    v_ref,
    att_ref,
    resid_ref,
    low_ref,
    gates_ref,
    gates_t_ref,
):
    x = x_ref[0].astype(F32)
    unit, _ = norm_parts(x)
    normed = (unit * vec_ref[0:1] + vec_ref[1:2]).astype(BF16)
    q_ref[0] = (dot(normed, wq_ref[...]) + vec_ref[2:3]).astype(BF16)
    k_ref[0] = dot(normed, wk_ref[...]).astype(BF16)
    v_ref[0] = (dot(normed, wv_ref[...]) + vec_ref[3:4]).astype(BF16)
    for j in range(HEADS // 2):
        cols = slice(j * PAIR, (j + 1) * PAIR)
        probs = pair_probs(stack_heads(q_ref[0, :, cols]), k_ref[0, :, cols], seq_len)
        mixed = merge_heads(dot(probs.astype(BF16), v_ref[0, :, cols]))
        att_ref[0, :, cols] = mixed.astype(BF16)
    resid = x + dot(att_ref[0], wo_ref[...]) + vec_ref[4:5]
    resid_ref[0] = resid
    unit_two, _ = norm_parts(resid)
    low = (unit_two * vec_ref[5:6] + vec_ref[6:7]).astype(BF16)
    low_ref[0] = low
    logits = dot(low, router_ref[...])
    powers = jnp.exp(logits - jnp.max(logits, axis=1, keepdims=True))
    gates = powers * (1.0 / jnp.sum(powers, axis=1, keepdims=True))
    gates_ref[0] = gates
    gates_t_ref[0] = gates.T


def run_forward(tokens, dense, vectors, router, seq_len):
    images, rows, width = tokens.shape
    experts = router.shape[1]

    def column(j):
        return pl.BlockSpec((width, width), lambda i: (0, j), pipeline_mode=pl.Buffered(1))

    big = jax.ShapeDtypeStruct((images, rows, width), BF16)
    return pl.pallas_call(
        functools.partial(forward_kernel, seq_len),
        grid=(images,),
        in_specs=[
            per_image(rows, width),
            column(0),
            column(1),
            column(2),
            column(3),
            whole(vectors.shape),
            whole(router.shape),
        ],
        out_specs=[per_image(rows, width)] * 6
        + [per_image(rows, experts), per_image(experts, rows)],
        out_shape=[big, big, big, big, jax.ShapeDtypeStruct(big.shape, F32), big]
        + [
            jax.ShapeDtypeStruct((images, rows, experts), F32),
            jax.ShapeDtypeStruct((images, experts, rows), F32),
        ],
        compiler_params=params(),
        cost_estimate=cost(18),
    )(tokens, dense, dense, dense, dense, vectors, router)


def dispatch_kernel(pos_ref, values_ref, *rest):
    expert = pl.program_id(0)
    images, rows, width = values_ref.shape
    gates_t_ref = rest[0] if len(rest) == 3 else None
    out_refs = rest[-2:] if gates_t_ref is not None else rest
    slots = sum(ref.shape[1] for ref in out_refs)
    half = slots // 2
    lanes = round_up(slots, 128)
    total = jnp.zeros((slots, width), F32)
    parts = jnp.zeros((8, lanes), F32)
    index = lax.broadcasted_iota(jnp.int32, (lanes, rows), 0)
    slot = jnp.where(index < slots, index + expert * slots, -2)
    for b in range(images):
        hit = (pos_ref[b, 0:1] == slot) | (pos_ref[b, 1:2] == slot)
        hit = jnp.where(hit, 1.0, 0.0).astype(BF16)
        total = total + dot(hit[:slots], values_ref[b])
        if gates_t_ref is not None:
            gate = jnp.broadcast_to(gates_t_ref[b, pl.ds(expert, 1)], (8, rows))
            high = gate.astype(BF16).astype(F32)
            middle = (gate - high).astype(BF16).astype(F32)
            part = lax.broadcasted_iota(jnp.int32, gate.shape, 0)
            split = jnp.where(
                part == 0,
                high,
                jnp.where(part == 1, middle, jnp.where(part == 2, gate - high - middle, 0.0)),
            )
            parts = parts + dot_nt(split.astype(BF16), hit)
    if gates_t_ref is None:
        out_refs[0][0] = total.astype(BF16)
        return
    tail = jnp.concatenate([parts, jnp.zeros((8, width - lanes), F32)], axis=1)
    out_refs[0][0] = jnp.concatenate([total[: half - 8], tail], axis=0).astype(BF16)
    out_refs[1][0] = total[half:].astype(BF16)


def run_dispatch(pos_rows, values, slots, experts, gates_t=None):
    width = values.shape[2]
    operands = (pos_rows, values) + (() if gates_t is None else (gates_t,))
    pieces = [slots] if gates_t is None else [slots // 2] * 2
    return pl.pallas_call(
        dispatch_kernel,
        grid=(experts,),
        in_specs=[whole(o.shape) for o in operands],
        out_specs=[pl.BlockSpec((1, piece, width), lambda i: (i, 0, 0)) for piece in pieces],
        out_shape=[jax.ShapeDtypeStruct((experts, piece, width), BF16) for piece in pieces],
        compiler_params=params(),
        cost_estimate=cost(7.5),
    )(*operands)


def gelu_parts(hidden):
    phi = 0.5 + 0.5 * lax.erf(hidden * (0.5**0.5))
    density = jnp.exp(hidden * hidden * -0.5) * 0.3989422804014327
    return hidden * phi, phi + hidden * density


def expert_forward_kernel(
    part,
    chunk,
    x_ref,
    cot_ref,
    picks_ref,
    up_ref,
    bias_up_ref,
    down_ref,
    bias_down_ref,
    *rest,
):
    carry_ref, before_ref = rest[:2] if len(rest) == 10 else (None, None)
    (
        result_ref,
        down_grad_ref,
        slope_ref,
        grad_ref,
        bias_grad_ref,
        total_ref,
        grad_t_ref,
        active_ref,
    ) = rest[-8:]
    step = pl.program_id(0)
    sources, slots, width = x_ref.shape
    rows = sources * slots
    lanes = picks_ref.shape[2]

    @pl.when(step == 0)
    def _():
        bias_grad = jnp.zeros((1, width), F32)
        for s in range(sources):
            parts = picks_ref[s].astype(F32)
            pick = jnp.broadcast_to(parts[0:1] + parts[1:2] + parts[2:3], (128, lanes)).T
            pick = pick[part * slots : (part + 1) * slots]
            pick = jnp.concatenate([pick] * (width // 128), axis=1)
            grad = (pick * cot_ref[s].astype(F32)).astype(BF16)
            grad_ref[s * slots : (s + 1) * slots, :] = grad
            bias_grad = bias_grad + jnp.sum(grad.astype(F32), axis=0, keepdims=True)
        bias_grad_ref[...] = bias_grad
        grad_t_ref[...] = grad_ref[...].T
        total_ref[...] = jnp.broadcast_to(bias_down_ref[...], total_ref.shape)

    x_flat = x_ref.reshape(rows, width)
    for r in range(rows // chunk):
        here = slice(r * chunk, (r + 1) * chunk)
        hidden = dot(x_flat[here, :], up_ref[...]) + bias_up_ref[...]
        active, slope = gelu_parts(hidden)
        active = active.astype(BF16)
        active_ref[here, :] = active
        slope_ref[here, :] = slope.astype(BF16)
        total_ref[here, :] += dot(active, down_ref[...])
    down_grad = dot(grad_t_ref[...], active_ref[...])
    if carry_ref is not None:
        down_grad = down_grad + carry_ref[0]
    down_grad_ref[0] = down_grad.astype(down_grad_ref.dtype)

    @pl.when(step == pl.num_programs(0) - 1)
    def _():
        result = total_ref[...].astype(BF16)
        if before_ref is None:
            result_ref[...] = result
            return
        for s in range(sources):
            here = slice(s * slots, (s + 1) * slots)
            result_ref[s, :slots] = before_ref[here, :]
            result_ref[s, slots:] = result[here]


def expert_backward_kernel(
    chunk,
    x_ref,
    x_more_ref,
    grad_ref,
    grad_more_ref,
    slope_ref,
    slope_more_ref,
    up_ref,
    down_ref,
    entry_ref,
    up_grad_ref,
    bias_grad_ref,
    total_ref,
    x_t_ref,
    hidden_grad_ref,
):
    step = pl.program_id(0)
    rows = grad_ref.shape[0]
    sources, slots, _ = entry_ref.shape
    half = slots // 2

    @pl.when(step == 0)
    def _():
        x_t_ref[:, :rows] = x_ref[...].T
        x_t_ref[:, rows:] = x_more_ref[...].T
        total_ref[...] = jnp.zeros_like(total_ref)

    bias_grad = jnp.zeros(bias_grad_ref.shape, F32)
    for part, (grads, slopes) in enumerate(((grad_ref, slope_ref), (grad_more_ref, slope_more_ref))):
        for r in range(rows // chunk):
            here = slice(r * chunk, (r + 1) * chunk)
            there = slice(part * rows + r * chunk, part * rows + (r + 1) * chunk)
            active_grad = dot_nt(grads[here, :], down_ref[...])
            hidden_grad = (active_grad * slopes[here, :].astype(F32)).astype(BF16)
            hidden_grad_ref[there, :] = hidden_grad
            bias_grad = bias_grad + jnp.sum(hidden_grad.astype(F32), axis=0, keepdims=True)
            total_ref[there, :] += dot_nt(hidden_grad, up_ref[...])
    bias_grad_ref[...] = bias_grad
    up_grad_ref[...] = dot(x_t_ref[...], hidden_grad_ref[...]).astype(BF16)

    @pl.when(step == pl.num_programs(0) - 1)
    def _():
        for part in range(2):
            for s in range(sources):
                place = part * rows + s * half
                entry_ref[s, part * half : (part + 1) * half] = total_ref[
                    place : place + half, :
                ].astype(BF16)


def chunk_of(rows):
    for size in (1024, 512, 256, 128, 64, 32):
        if rows % size == 0:
            return size
    return rows


def run_experts_forward(part, x, cot, picks, w_up, b_up, w_down, b_down, parts, earlier=None):
    sources, slots, width = x.shape
    rows = sources * slots
    result_shape = (rows, width) if earlier is None else (sources, 2 * slots, width)
    units = w_up.shape[1]
    tile = units // parts
    carried = pl.BlockSpec((1, width, tile), lambda i: (i, 0, 0))
    return pl.pallas_call(
        functools.partial(expert_forward_kernel, part, chunk_of(rows)),
        grid=(parts,),
        in_specs=[
            whole(x.shape),
            pl.BlockSpec(x.shape, lambda i: (0, part, 0), pipeline_mode=pl.Buffered(1)),
            whole(picks.shape),
            pl.BlockSpec((width, tile), lambda i: (0, i)),
            pl.BlockSpec((1, tile), lambda i: (0, i)),
            pl.BlockSpec((tile, width), lambda i: (i, 0)),
            whole((1, width)),
        ]
        + ([] if earlier is None else [carried, whole((rows, width))]),
        out_specs=[
            whole(result_shape),
            carried,
            pl.BlockSpec((rows, tile), lambda i: (0, i)),
            whole((rows, width)),
            whole((1, width)),
        ],
        out_shape=[
            jax.ShapeDtypeStruct(result_shape, BF16),
            jax.ShapeDtypeStruct((parts, width, tile), F32 if earlier is None else BF16),
            jax.ShapeDtypeStruct((rows, units), BF16),
            jax.ShapeDtypeStruct((rows, width), BF16),
            jax.ShapeDtypeStruct((1, width), F32),
        ],
        scratch_shapes=[
            pltpu.VMEM((rows, width), F32),
            pltpu.VMEM((width, rows), BF16),
            pltpu.VMEM((rows, tile), BF16),
        ],
        compiler_params=params(),
        cost_estimate=cost(24),
    )(x, cot, picks, w_up, b_up, w_down, b_down, *(() if earlier is None else earlier))


def run_experts_backward(x, grad, slope, w_up, w_down, sources, parts):
    rows, width = x[0].shape
    units = w_up.shape[1]
    tile = units // parts
    entry_shape = (sources, 2 * rows // sources, width)
    return pl.pallas_call(
        functools.partial(expert_backward_kernel, min(chunk_of(rows), 512)),
        grid=(parts,),
        in_specs=[whole((rows, width))] * 4
        + [pl.BlockSpec((rows, tile), lambda i: (0, i))] * 2
        + [
            pl.BlockSpec((width, tile), lambda i: (0, i)),
            pl.BlockSpec((tile, width), lambda i: (i, 0)),
        ],
        out_specs=[
            whole(entry_shape),
            pl.BlockSpec((width, tile), lambda i: (0, i)),
            pl.BlockSpec((1, tile), lambda i: (0, i)),
        ],
        out_shape=[
            jax.ShapeDtypeStruct(entry_shape, BF16),
            jax.ShapeDtypeStruct((width, units), BF16),
            jax.ShapeDtypeStruct((1, units), F32),
        ],
        scratch_shapes=[
            pltpu.VMEM((2 * rows, width), F32),
            pltpu.VMEM((width, 2 * rows), BF16),
            pltpu.VMEM((2 * rows, tile), BF16),
        ],
        compiler_params=params(),
        cost_estimate=cost(40),
    )(*x, *grad, *slope, w_up, w_down)


def gather_slots(places, values_ref):
    slot = lax.broadcasted_iota(jnp.int32, (places[0].shape[0], values_ref.shape[0]), 1)
    hit = places[0] == slot
    for place in places[1:]:
        hit = hit | (place == slot)
    return dot(jnp.where(hit, 1.0, 0.0).astype(BF16), values_ref[...])


def combine_kernel(
    seq_len,
    returned_ref,
    pos_ref,
    routes_ref,
    gates_ref,
    resid_ref,
    cot_ref,
    low_ref,
    x_ref,
    q_ref,
    k_ref,
    att_ref,
    vec_ref,
    router_t_ref,
    mixed_ref,
    low_grad_ref,
    router_grad_ref,
    probs_ref,
    probs_t_ref,
    normed_t_ref,
    att_t_ref,
):
    rows, experts = gates_ref.shape[1:]

    @pl.when(pl.program_id(0) == 0)
    def _():
        router_grad_ref[...] = jnp.zeros_like(router_grad_ref)

    for j in range(HEADS // 2):
        cols = slice(j * PAIR, (j + 1) * PAIR)
        probs = pair_probs(stack_heads(q_ref[0, :, cols]), k_ref[0, :, cols], seq_len)
        probs_ref[0, j] = probs
        probs_t_ref[0, j] = probs.astype(BF16).T
    unit, _ = norm_parts(x_ref[0].astype(F32))
    normed_t_ref[0] = (unit * vec_ref[0:1] + vec_ref[1:2]).astype(BF16).T
    att_t_ref[0] = att_ref[0].T

    gates = gates_ref[0]
    upstream = cot_ref[0].astype(F32)
    expert = lax.broadcasted_iota(jnp.int32, (rows, experts), 1)
    output = resid_ref[0]
    gate_grad = jnp.zeros((rows, experts), F32)
    for k in range(2):
        picked = gather_slots([pos_ref[0, :, k : k + 1]], returned_ref)
        chosen = routes_ref[0, :, k : k + 1] == expert
        pick = jnp.sum(jnp.where(chosen, gates, 0.0), axis=1, keepdims=True)
        output = output + pick * picked
        pick_grad = jnp.sum(picked * upstream, axis=1, keepdims=True)
        gate_grad = gate_grad + jnp.where(chosen, pick_grad, 0.0)
    mixed_ref[0] = output.astype(BF16)[:seq_len]
    logit_grad = gates * (gate_grad - jnp.sum(gates * gate_grad, axis=1, keepdims=True))
    low_grad_ref[0] = jnp.dot(logit_grad, router_t_ref[...], precision=HIGHEST)
    router_grad_ref[...] += lax.dot_general(
        logit_grad,
        low_ref[0].astype(F32),
        (((0,), (0,)), ((), ())),
        precision=HIGHEST,
        preferred_element_type=F32,
    )


def run_combine(
    returned, pos_cols, routes_cols, gates, resid, cot, low, x, query, key,
    attended, vectors, router_t, seq_len,
):
    images, rows, width = resid.shape
    experts = gates.shape[2]
    pairs = HEADS // 2
    return pl.pallas_call(
        functools.partial(combine_kernel, seq_len),
        grid=(images,),
        in_specs=[
            whole(returned.shape),
            per_image(rows, 2),
            per_image(rows, 2),
            per_image(rows, experts),
        ]
        + [per_image(rows, width)] * 7
        + [whole(vectors.shape), whole(router_t.shape)],
        out_specs=[
            per_image(seq_len, width),
            per_image(rows, width),
            whole((experts, width)),
            per_image(pairs, 2 * rows, rows),
            per_image(pairs, rows, 2 * rows),
            per_image(width, rows),
            per_image(width, rows),
        ],
        out_shape=[
            jax.ShapeDtypeStruct((images, seq_len, width), BF16),
            jax.ShapeDtypeStruct((images, rows, width), F32),
            jax.ShapeDtypeStruct((experts, width), F32),
            jax.ShapeDtypeStruct((images, pairs, 2 * rows, rows), F32),
            jax.ShapeDtypeStruct((images, pairs, rows, 2 * rows), BF16),
            jax.ShapeDtypeStruct((images, width, rows), BF16),
            jax.ShapeDtypeStruct((images, width, rows), BF16),
        ],
        compiler_params=params(),
        cost_estimate=cost(20),
    )(
        returned, pos_cols, routes_cols, gates, resid, cot, low, x, query, key,
        attended, vectors, router_t,
    )


def branch_kernel(
    entry_ref,
    pos_ref,
    low_grad_ref,
    resid_ref,
    cot_ref,
    probs_ref,
    probs_t_ref,
    q_ref,
    k_ref,
    v_ref,
    normed_t_ref,
    att_t_ref,
    wo_ref,
    wq_ref,
    wk_ref,
    wv_ref,
    columns_ref,
    vec_ref,
    router_grad_ref,
    resid_grad_ref,
    dq_ref,
    dk_ref,
    dv_ref,
    first_ref,
    second_ref,
    first_sum_ref,
    second_sum_ref,
    small_ref,
):
    image = pl.program_id(0)
    rows, width = resid_ref.shape[1:]

    @pl.when(image == 0)
    def _():
        first_sum_ref[...] = jnp.zeros_like(first_sum_ref)
        second_sum_ref[...] = jnp.zeros_like(second_sum_ref)
        small_ref[...] = jnp.zeros_like(small_ref)

    def add_small(row, values):
        small_ref[row : row + 1, :] += jnp.sum(values, axis=0, keepdims=True)

    low_grad = low_grad_ref[0] + gather_slots(
        [pos_ref[0, :, 0:1], pos_ref[0, :, 1:2]], entry_ref
    )
    unit, inverse = norm_parts(resid_ref[0])
    add_small(5, low_grad * unit)
    add_small(6, low_grad)
    resid_grad = cot_ref[0].astype(F32) + norm_pull(unit, inverse, vec_ref[5:6], low_grad)
    resid_grad_ref[0] = resid_grad
    branch_grad = resid_grad.astype(BF16)
    add_small(4, branch_grad.astype(F32))
    second_sum_ref[:, width:] += dot(att_t_ref[0], branch_grad)
    att_grad = dot_nt(branch_grad, wo_ref[...]).astype(BF16)
    for j in range(HEADS // 2):
        cols = slice(j * PAIR, (j + 1) * PAIR)
        query_stack = stack_heads(q_ref[0, :, cols])
        key_pair = k_ref[0, :, cols]
        probs = probs_ref[0, j]
        grad_stack = stack_heads(att_grad[:, cols])
        dv_ref[0, :, cols] = dot(probs_t_ref[0, j], grad_stack).astype(BF16)
        probs_grad = dot_nt(grad_stack, v_ref[0, :, cols])
        score_grad = probs * (
            probs_grad - jnp.sum(probs * probs_grad, axis=1, keepdims=True)
        )
        score_grad = score_grad.astype(BF16)
        dq_ref[0, :, cols] = (merge_heads(dot(score_grad, key_pair)) * SCALE).astype(BF16)
        dk_ref[0, :, cols] = (dot_tn(score_grad, query_stack) * SCALE).astype(BF16)
    dq, dk, dv = dq_ref[0], dk_ref[0], dv_ref[0]
    add_small(2, dq.astype(F32))
    add_small(3, dv.astype(F32))
    add_small(7, dk.astype(F32))
    normed_t = normed_t_ref[0]
    first_sum_ref[:, :width] += dot(normed_t, dq)
    first_sum_ref[:, width:] += dot(normed_t, dk)
    second_sum_ref[:, :width] += dot(normed_t, dv)

    @pl.when(image == pl.num_programs(0) - 1)
    def _():
        first_ref[...] = first_sum_ref[...].astype(BF16)
        second_ref[:, : 2 * width] = second_sum_ref[...].astype(BF16)
        gain = 1.0 / columns_ref[:, 0:1].astype(F32)
        shift = columns_ref[:, 1:2].astype(F32)
        gain_grad = jnp.zeros((width, 1), F32)
        shift_grad = jnp.zeros((width, 1), F32)
        for weight_ref, sum_ref, start, row in (
            (wq_ref, first_sum_ref, 0, 2),
            (wk_ref, first_sum_ref, width, 7),
            (wv_ref, second_sum_ref, 0, 3),
        ):
            weight = weight_ref[...].astype(F32)
            bias = small_ref[row : row + 1, :]
            scaled = sum_ref[:, start : start + width] - shift * bias
            gain_grad = gain_grad + jnp.sum(weight * scaled, axis=1, keepdims=True)
            shift_grad = shift_grad + jnp.sum(weight * bias, axis=1, keepdims=True)
        narrow = jnp.concatenate([small_ref[...], router_grad_ref[...]], axis=0)
        narrow = jnp.concatenate(
            [narrow, jnp.zeros((128 - narrow.shape[0], width), F32)], axis=0
        ).T
        lane = lax.broadcasted_iota(jnp.int32, narrow.shape, 1)
        narrow = jnp.where(lane == 0, gain_grad * gain, jnp.where(lane == 1, shift_grad, narrow))
        second_ref[:, 2 * width :] = narrow.astype(BF16)


def run_branch(
    entry, pos_cols, low_grad, resid, cot, probs, probs_t, query, key, value,
    normed_t, att_t, dense, vectors, router_grad,
):
    images, rows, width = resid.shape
    pairs = HEADS // 2
    wide = (width, 2 * width)
    wider = (width, 2 * width + 128)

    def column(j):
        return pl.BlockSpec((width, width), lambda i: (0, j), pipeline_mode=pl.Buffered(1))

    low_shape = jax.ShapeDtypeStruct((images, rows, width), BF16)
    return pl.pallas_call(
        branch_kernel,
        grid=(images,),
        in_specs=[whole(entry.shape), per_image(rows, 2)]
        + [per_image(rows, width)] * 3
        + [per_image(pairs, 2 * rows, rows), per_image(pairs, rows, 2 * rows)]
        + [per_image(rows, width)] * 3
        + [per_image(width, rows)] * 2
        + [
            column(3),
            column(0),
            column(1),
            column(2),
            pl.BlockSpec(
                (width, 128), lambda i: (0, 4 * width // 128), pipeline_mode=pl.Buffered(1)
            ),
            whole(vectors.shape),
            whole(router_grad.shape),
        ],
        out_specs=[per_image(rows, width)] * 4 + [whole(wide), whole(wider)],
        out_shape=[
            jax.ShapeDtypeStruct((images, rows, width), F32),
            low_shape,
            low_shape,
            low_shape,
            jax.ShapeDtypeStruct(wide, BF16),
            jax.ShapeDtypeStruct(wider, BF16),
        ],
        scratch_shapes=[
            pltpu.VMEM(wide, F32),
            pltpu.VMEM(wide, F32),
            pltpu.VMEM((8, width), F32),
        ],
        compiler_params=params(),
        cost_estimate=cost(36),
    )(
        entry, pos_cols, low_grad, resid, cot, probs, probs_t, query, key, value,
        normed_t, att_t, dense, dense, dense, dense, dense, vectors, router_grad,
    )


def input_kernel(
    dq_ref, dk_ref, dv_ref, wq_ref, wk_ref, wv_ref, x_ref, resid_grad_ref, vec_ref, x_grad_ref
):
    seq_len = x_grad_ref.shape[1]
    unit, inverse = norm_parts(x_ref[0].astype(F32))
    normed_grad = (
        dot_nt(dq_ref[0], wq_ref[...])
        + dot_nt(dk_ref[0], wk_ref[...])
        + dot_nt(dv_ref[0], wv_ref[...])
    )
    x_grad = resid_grad_ref[0] + norm_pull(unit, inverse, vec_ref[0:1], normed_grad)
    x_grad_ref[0] = x_grad[:seq_len]


def run_input(dq, dk, dv, dense, x, resid_grad, vectors, seq_len):
    images, rows, width = x.shape

    def column(j):
        return pl.BlockSpec((width, width), lambda i: (0, j), pipeline_mode=pl.Buffered(1))

    return pl.pallas_call(
        input_kernel,
        grid=(images,),
        in_specs=[per_image(rows, width)] * 3
        + [column(0), column(1), column(2)]
        + [per_image(rows, width)] * 2
        + [whole(vectors.shape)],
        out_specs=per_image(seq_len, width),
        out_shape=jax.ShapeDtypeStruct((images, seq_len, width), F32),
        compiler_params=params(),
        cost_estimate=cost(10),
    )(dq, dk, dv, dense, dense, dense, x, resid_grad, vectors)


def bits_of(size):
    return [1 << i for i in range(size.bit_length() - 1)]


def swap(values, axis, bit):
    return lax.ppermute(values, axis, [(i, i ^ bit) for i in range(lax.axis_size(axis))])


def my_bit(axis, bit):
    return (lax.axis_index(axis) // bit) % 2


def plane_bits():
    return bits_of(lax.axis_size("expert"))[1:]


def expert_bits():
    return bits_of(lax.axis_size("expert"))[::-1]


def gather_line(shard, axis):
    count, me = lax.axis_size(axis), lax.axis_index(axis)
    got = [
        lax.ppermute(shard, axis, [(i, (i + k) % count) for i in range(count)])
        for k in range(count - 1, 0, -1)
    ]
    ring = jnp.stack((got + [shard]) * 2)
    return lax.dynamic_slice_in_dim(ring, count - 1 - me, count, 0)


def gather_plane(shard):
    chips = lax.axis_size("expert") // 2
    got = [shard] + [swap(shard, "expert", 2 * k) for k in range(1, chips)]
    out = jnp.stack(got, axis=1)
    for bit in bits_of(chips):
        cut = out.reshape((out.shape[0], chips // (2 * bit), 2, bit) + out.shape[2:])
        turned = jnp.where(my_bit("expert", 2 * bit) == 1, cut[:, :, ::-1], cut)
        out = turned.reshape(out.shape)
    return out


def gather_core(shard):
    other = swap(shard, "expert", 1)
    mine_low = my_bit("expert", 1) == 0
    both = jnp.stack(
        [jnp.where(mine_low, shard, other), jnp.where(mine_low, other, shard)], axis=2
    )
    return both.reshape(-1, shard.shape[-1])


def scatter_line(total, axis):
    count, me = lax.axis_size(axis), lax.axis_index(axis)
    kept = lax.dynamic_index_in_dim(total, me, 0, keepdims=False).astype(F32)
    for k in range(1, count):
        sent = lax.dynamic_index_in_dim(total, (me + k) % count, 0, keepdims=False)
        got = lax.ppermute(sent, axis, [(i, (i + k) % count) for i in range(count)])
        kept = kept + got.astype(F32)
    return kept


def scatter_start(total):
    dims = expert_bits()
    return total.reshape((lax.axis_size("dp"),) + (2,) * len(dims) + (-1, total.shape[-1])), dims


def scatter_bits(state, bits):
    total, dims = state
    dims = list(dims)
    for bit in bits:
        place = dims.index(bit) + 1
        mine = my_bit("expert", bit)
        sent = lax.dynamic_index_in_dim(total, 1 - mine, place, keepdims=False)
        kept = lax.dynamic_index_in_dim(total, mine, place, keepdims=False)
        total = (kept.astype(F32) + swap(sent, "expert", bit).astype(F32)).astype(total.dtype)
        dims.remove(bit)
    return total, dims


def exchange(values):
    return lax.all_to_all(values, "expert", split_axis=0, concat_axis=0, tiled=True)


def exchange_after(values, earlier):
    if earlier is not None:
        values, _ = lax.optimization_barrier((values, earlier))
    return exchange(values)


def per_device(
    tokens,
    routes,
    gain_one,
    shift_one,
    w_query,
    b_query,
    w_key,
    w_value,
    b_value,
    w_out,
    b_out,
    gain_two,
    shift_two,
    w_router,
    w_up,
    b_up,
    w_down,
    b_down,
    cotangent,
):
    images, seq_len, width = tokens.shape
    token_rows = images * seq_len
    parts = lax.axis_size("dp")
    experts = w_up.shape[0] * lax.axis_size("expert")
    capacity = max((token_rows * 10 // (4 * experts) + 7) // 8 * 8, 8)
    slots = round_up(capacity + 8, 32)
    half = slots // 2
    lanes = round_up(slots, 128)
    rows = round_up(seq_len, 16)
    pad = ((0, 0), (0, rows - seq_len), (0, 0))

    vectors = (gain_one, shift_one, b_query, b_value, b_out, gain_two, shift_two)
    spare = jnp.zeros((w_query.shape[0], 128 - len(vectors) - experts), BF16)
    small = jnp.concatenate([jnp.stack(vectors, axis=1), w_router, spare], axis=1)
    shard = jnp.concatenate([w_query, w_key, w_value, w_out, small], axis=1)
    shard = gather_line(shard, "dp")

    flat_routes = routes.reshape(-1)
    table = (flat_routes[:, None] == jnp.arange(experts, dtype=jnp.int32)[None, :]).astype(
        jnp.int32
    )
    before = jnp.cumsum(table, axis=0) - table
    slot = jnp.sum(before * table, axis=1)
    slot = jnp.where(slot < half - 8, slot, slot + 8)
    pos_cols = (flat_routes * slots + slot).reshape(images, seq_len, 2)
    pos_cols = jnp.pad(pos_cols, pad, constant_values=-1)
    pos_rows = pos_cols.transpose(0, 2, 1)
    routes_cols = jnp.pad(routes, pad, constant_values=-1)

    x = jnp.pad(tokens, pad)
    cot = jnp.pad(cotangent, pad)
    shard, pos_sent, x = lax.optimization_barrier((shard, pos_rows, x))
    shard = gather_plane(shard)
    (cot_sent,) = run_dispatch(pos_sent, cot, slots, experts)
    shard, cot_sent, x = lax.optimization_barrier((shard, cot_sent, x))
    cot_here = exchange(cot_sent)
    dense = gather_core(shard)
    small = dense[:, 4 * width :]
    vectors = jnp.pad(small[:, : len(vectors)].T.astype(F32), ((0, 8 - len(vectors)), (0, 0)))
    router = small[:, 7 : 7 + experts]
    router_t = router.T.astype(F32)

    query, key, value, attended, resid, low, gates, gates_t = run_forward(
        x, dense, vectors, router, seq_len
    )
    up, down = w_up[0], w_down[0]
    bias_up, bias_down = b_up.astype(F32), b_down.astype(F32)
    low_sent = run_dispatch(pos_rows, low, slots, experts, gates_t)
    low_here, sent = [], cot_here
    for piece in low_sent:
        sent = exchange_after(piece, sent)
        low_here.append(sent)
    picks = low_here[0][:, half - 8 :, :lanes]
    forward, earlier = [], None
    for i in range(2):
        step = run_experts_forward(
            i, low_here[i], cot_here, picks, up, bias_up, down, bias_down, parts, earlier
        )
        earlier = (step[1], step[0])
        forward.append(step)
    result, down_grad = forward[1][:2]
    returned = exchange_after(result, sent)
    down_shard = lax.psum_scatter(down_grad, "dp", scatter_dimension=0, tiled=True)
    entry, up_grad, bias_up_grad = run_experts_backward(
        [piece.reshape(-1, width) for piece in low_here],
        [step[3] for step in forward],
        [step[2] for step in forward],
        up,
        down,
        experts,
        parts,
    )
    entry_back = exchange_after(entry, returned)
    up_shard = lax.psum_scatter(up_grad, "dp", scatter_dimension=0, tiled=True)
    bias_down_grad = forward[0][4] + forward[1][4]
    biases = jnp.concatenate(
        [bias_up_grad.reshape(parts, -1), bias_down_grad.reshape(parts, -1)], axis=1
    )
    biases = scatter_line(biases, "dp")[None]
    mixed, low_grad, router_grad, probs, probs_t, normed_t, att_t = run_combine(
        returned.reshape(-1, width),
        pos_cols,
        routes_cols,
        gates,
        resid,
        cot,
        low,
        x,
        query,
        key,
        attended,
        vectors,
        router_t,
        seq_len,
    )
    entry_back, biases = lax.optimization_barrier((entry_back, biases))
    resid_grad, dq, dk, dv, first_grad, second_grad = run_branch(
        entry_back.reshape(-1, width),
        pos_cols,
        low_grad,
        resid,
        cot,
        probs,
        probs_t,
        query,
        key,
        value,
        normed_t,
        att_t,
        dense,
        vectors,
        router_grad,
    )
    others = plane_bits()
    down_shard = down_shard.transpose(0, 2, 1).astype(F32)
    first_grad = scatter_bits(scatter_start(first_grad), [1])
    second_grad = scatter_bits(scatter_start(second_grad), [1])
    first_part, second_part, dv = lax.optimization_barrier((first_grad[0], second_grad[0], dv))
    first_grad = scatter_bits((first_part, first_grad[1]), others[-1:])
    second_grad = scatter_bits((second_part, second_grad[1]), others[:1])
    x_grad = run_input(dq, dk, dv, dense, x, resid_grad, vectors, seq_len)
    first_part, second_part, x_grad, down_shard = lax.optimization_barrier(
        (first_grad[0], second_grad[0], x_grad, down_shard)
    )
    first_grad = scatter_bits((first_part, first_grad[1]), others[:-1][::-1])
    second_grad = scatter_bits((second_part, second_grad[1]), others[1:])
    dense_shard = jnp.concatenate([first_grad[0], second_grad[0]], axis=2)
    dense_shard = scatter_line(dense_shard, "dp")
    up_shard, dense_shard = lax.optimization_barrier((up_shard, dense_shard))
    columns = dense_shard[:, 4 * width :]
    tile = down_shard.shape[1]
    return (
        mixed,
        x_grad,
        columns[:, 0],
        columns[:, 1],
        dense_shard[:, :width],
        columns[:, 2],
        dense_shard[:, width : 2 * width],
        dense_shard[:, 2 * width : 3 * width],
        columns[:, 3],
        dense_shard[:, 3 * width : 4 * width],
        columns[:, 4],
        columns[:, 5],
        columns[:, 6],
        columns[:, 8 : 8 + experts],
        up_shard.astype(F32)[None],
        biases[:, :tile],
        down_shard,
        biases[:, tile:],
    )


def solution(mesh):
    both = ("dp", "expert")
    row, matrix, cube = P(both), P(both, None), P(both, None, None)
    return jax.shard_map(
        per_device,
        mesh=mesh,
        in_specs=(
            cube, cube, row, row, matrix, row, matrix, matrix, row, matrix, row, row, row, matrix,
            P("expert", None, None),
            P("expert", None),
            P("expert", None, None),
            P("expert", None),
            cube,
        ),
        out_specs=(
            cube, cube, row, row, matrix, row, matrix, matrix, row, matrix, row, row, row, matrix,
            P("expert", "dp", None),
            P("expert", "dp"),
            P("expert", "dp", None),
            P("expert", "dp"),
        ),
        check_vma=False,
    )
```
